32 devices in a mesh: groups: 2 (over y), frame: 4 (over z), space: 2 (over x), head: 2 (over core).
Axes of the slice: x: 2, y: 2, z: 4, core: 2. Of those that a mesh axis runs over, the one named last changes fastest.
Arguments:
- queries: bfloat16 [8, 512, 3072], P(('groups', 'frame'), 'space', 'head'), parts along dimension 0, may hold values from -6 to 6
- key_states: bfloat16 [8, 512, 3072], P(('groups', 'frame'), 'space', 'head'), parts along dimension 0, may hold values from -24 to 24
- value_states: bfloat16 [8, 512, 3072], P(('groups', 'frame'), 'space', 'head'), parts along dimension 0, may hold values from -6 to 6
- profile: int32 [24], replicated, may hold values from 0 to 1, as said below
- window: int32 [24], replicated, may hold values from 1 to 4, as said below
Outputs:
- attended: bfloat16 [8, 512, 3072], P(('groups', 'frame'), 'space', 'head'), parts along dimension 0
The draws below stay inside these ranges and needn't reach their ends.
There are 2 independent parts, one for each index of `groups`. The reference program is written for one: setup_inputs(seed, part) draws one part's arguments, and reference() takes and returns one part's arrays. A program takes and returns all parts, laid end to end along the dimension named above; an argument that names none is the same for every part. Nothing has to cross between parts.
Inputs may be any that keep to these rules, and one draw needn't show every extreme that they name: `profile`: 1 marks a head of frame-local attention, 0 a head of attention over a window of frames; exactly half of the 24 heads are marked 1. Some head marked 0 in profile has window 4.
All inputs are finite; a program needn't handle non-finite values.
Results may differ from the reference program's by a relative error of at most 0.0055.
Values may be sent and summed in bfloat16 or wider, within the bound.
No kernel may reach another device: no remote copies, remote signals or barrier semaphores. Data moves between devices by JAX's collectives and lax.ppermute only.
A program may use at most 64 MiB of HBM per device.

```python
import jax
import jax.numpy as jnp
from jax import lax

H = 24
HD = 128
WMAX = 4
NTOK = 512
FRAMES = 4


def drawn_pair(key):
    base = jax.random.fold_in(key, 7)
    key_query, key_keys = jax.random.split(base, 2)
    shape_full = (FRAMES, NTOK, H * HD)
    query_draw = jnp.clip(jax.random.normal(key_query, shape_full, jnp.float32), -6.0, 6.0)
    key_draw = jnp.clip(jax.random.normal(key_keys, shape_full, jnp.float32), -6.0, 6.0)
    return (query_draw, key_draw)


def draw_queries(key, part):
    return drawn_pair(key)[0].astype(jnp.bfloat16)


def draw_key_states(key, part):
    return drawn_pair(key)[1].astype(jnp.bfloat16)


def head_classes(key):
    order = jax.random.permutation(jax.random.fold_in(key, 11), H)
    return (order < H // 2).astype(jnp.int32)


def draw_profile(key, part):
    return head_classes(key)


def draw_window(key, part):
    classes = head_classes(key)
    reaches = jax.random.randint(jax.random.fold_in(key, 13), (H,), 1, WMAX + 1)
    first_window = jnp.argmin(classes)
    return reaches.at[first_window].set(WMAX).astype(jnp.int32)


def level_of(rng, dims, cuts, low, high):
    def one(dim, parts):
        heights = jax.random.uniform(jax.random.fold_in(jax.random.fold_in(rng, 6), dim), (parts,), jnp.float32, low / len(cuts), high / len(cuts))
        return jnp.repeat(jnp.exp(heights), dims[dim] // parts).reshape((-1,) + (1,) * (len(dims) - dim - 1))

    loudness = one(*cuts[0])
    for cut in cuts[1:]:
        loudness = loudness * one(*cut)
    return loudness


def normal_values(key, shape, spread, bound, pieces=(), kind=jnp.bfloat16):
    drawn = jax.random.normal(key, shape, jnp.float32) * spread
    if len(pieces) > 0:
        drawn = level_of(key, shape, pieces, -0.22, 0.18) * drawn
    return jnp.clip(drawn, min=-bound, max=bound).astype(kind)


def setup_inputs(seed: int = 0, part: int = 0) -> dict:
    streams_of = jax.random.split(jax.random.key(seed), 6)
    part_splits = jax.random.split(jax.random.fold_in(streams_of[5], part), 6)
    return {
        "queries": draw_queries(jax.random.fold_in(jax.random.fold_in(streams_of[5], part), 71), part),
        "key_states": draw_key_states(jax.random.fold_in(jax.random.fold_in(streams_of[5], part), 71), part),
        "value_states": normal_values(part_splits[2], (FRAMES, NTOK, H * HD), 1.0, 6.0, ((0, 4), (1, 2), (2, 2))),
        "profile": draw_profile(jax.random.fold_in(streams_of[5], 71), part),
        "window": draw_window(jax.random.fold_in(streams_of[5], 71), part),
    }


def spatial_frames(queries, key_states, value_states):
    token_count = queries.shape[1]
    scale = HD ** -0.5

    def one_frame(item):
        query_frame, key_frame, value_frame = item
        query_heads = jnp.moveaxis(query_frame.reshape(token_count, H, HD), 1, 0)
        key_heads = jnp.moveaxis(key_frame.reshape(token_count, H, HD), 1, 0)
        value_heads = jnp.moveaxis(value_frame.reshape(token_count, H, HD), 1, 0)

        def one_head(triple):
            query_one, key_one, value_one = triple
            scores = jnp.dot(query_one, key_one.T, preferred_element_type=jnp.float32) * scale
            peak = jnp.max(scores, axis=1, keepdims=True)
            weights = jnp.exp(scores - peak)
            denominator = jnp.sum(weights, axis=1, keepdims=True)
            numerator = jnp.dot(weights.astype(jnp.bfloat16), value_one, preferred_element_type=jnp.float32)
            return numerator / denominator

        result = lax.map(one_head, (query_heads, key_heads, value_heads))
        return jnp.moveaxis(result, 0, 1)

    return lax.map(one_frame, (queries, key_states, value_states))


def temporal_frames(queries, key_states, value_states, window):
    frame_count, token_count = queries.shape[0], queries.shape[1]
    scale = HD ** -0.5
    shape_four = (frame_count, token_count, H, HD)
    query_heads = queries.reshape(shape_four).astype(jnp.float32)
    padding = ((WMAX, WMAX), (0, 0), (0, 0), (0, 0))
    key_padded = jnp.pad(key_states.reshape(shape_four), padding)
    value_padded = jnp.pad(value_states.reshape(shape_four), padding)
    frame_ids = jnp.arange(frame_count, dtype=jnp.int32)
    score_list = []
    for offset in range(-WMAX, WMAX + 1):
        near_keys = key_padded[WMAX + offset:WMAX + offset + frame_count]
        raw_scores = jnp.einsum("fnhd,fnhd->fnh", query_heads, near_keys.astype(jnp.float32)) * scale
        in_range = (frame_ids + offset >= 0) & (frame_ids + offset < frame_count)
        inside = in_range[:, None, None] & (window >= abs(offset))[None, None, :]
        score_list.append(jnp.where(inside, raw_scores, -1e30))
    scores = jnp.stack(score_list)
    peak = jnp.max(scores, axis=0)
    weights = jnp.exp(scores - peak[None])
    denominator = jnp.sum(weights, axis=0)
    rounded = weights.astype(jnp.bfloat16).astype(jnp.float32)
    numerator = jnp.zeros(shape_four, jnp.float32)
    for index, offset in enumerate(range(-WMAX, WMAX + 1)):
        near_values = value_padded[WMAX + offset:WMAX + offset + frame_count].astype(jnp.float32)
        numerator = numerator + rounded[index][..., None] * near_values
    return numerator / denominator[..., None]


def reference(queries, key_states, value_states, profile, window):
    spatial_part = spatial_frames(queries, key_states, value_states)
    temporal_part = temporal_frames(queries, key_states, value_states, window)
    chosen = jnp.where((profile == 1)[None, None, :, None], spatial_part, temporal_part)
    return chosen.reshape(queries.shape).astype(jnp.bfloat16)
```

```python
import functools

import jax
import jax.numpy as jnp
from jax import lax
from jax.experimental import pallas as pl
from jax.experimental.pallas import tpu as pltpu
from jax.sharding import PartitionSpec as P

HD = 128
HBM = pl.BlockSpec(memory_space=pl.ANY)
SMALL = pl.BlockSpec(memory_space=pltpu.SMEM)
FAST = pl.BlockSpec(memory_space=pltpu.VMEM)
SCALE = HD ** (-0.5)


def list_heads(profile, order, kind, width):
    first = lax.axis_index("head") * width

    def clear(i, carry):
        order[i] = 0
        return carry

    def step(i, count):
        hit = profile[first + i] == kind

        @pl.when(hit)
        def _():
            order[count] = i

        return count + hit.astype(jnp.int32)

    lax.fori_loop(0, width, clear, 0)
    return lax.fori_loop(0, width, step, 0)


def columns_of(head):
    return pl.ds(pl.multiple_of(head * HD, HD), HD)


def params(megabytes=40):
    return pltpu.CompilerParams(vmem_limit_bytes=megabytes << 20)


def pack_chunks(low, profile, query, key, value, *rest):
    *sends, order, sems = rest
    frames = len(sends) + 1
    width = query.shape[1] // HD
    slots, chunk = sends[0].shape[0], sends[0].shape[2]
    mine = lax.axis_index("frame")
    total = list_heads(profile, order, 0, width)

    @pl.when(total > low)
    def _():
        def one(slot, carry):
            columns = columns_of(order[low + slot])
            for distance, send in enumerate(sends, 1):
                to = lax.rem(mine + distance, frames)
                rows = pl.ds(pl.multiple_of(to * chunk, chunk), chunk)
                for index, source in enumerate((query, key, value)):
                    pltpu.make_async_copy(
                        source.at[rows, columns], send.at[slot, index], sems.at[distance - 1]
                    ).start()
            return carry

        lax.fori_loop(0, slots, one, 0)
        for distance, send in enumerate(sends, 1):
            pltpu.make_async_copy(send, send, sems.at[distance - 1]).wait()


def pack_rows(profile, key, value, send, order, sem):
    width = key.shape[1] // HD
    list_heads(profile, order, 1, width)

    def one(slot, carry):
        columns = columns_of(order[slot])
        for index, source in enumerate((key, value)):
            pltpu.make_async_copy(source.at[:, columns], send.at[slot, index], sem).start()
        return carry

    lax.fori_loop(0, send.shape[0], one, 0)
    pltpu.make_async_copy(send, send, sem).wait()


def spatial_heads(peers, profile, query, key, value, *rest):
    fetched, (out, order) = rest[:peers], rest[peers:]
    width = query.shape[1] // HD
    total = list_heads(profile, order, 1, width)

    def one(slot, carry):
        columns = columns_of(order[slot])
        keys = jnp.concatenate([key[:, columns]] + [f[slot, 0] for f in fetched])
        values = jnp.concatenate([value[:, columns]] + [f[slot, 1] for f in fetched])
        out[:, columns] = attend(query[:, columns], keys, values, None).astype(out.dtype)
        return carry

    lax.fori_loop(0, jnp.minimum(total, fetched[0].shape[0]) if peers else total, one, 0)


def attend(query, keys, values, inside):
    scores = lax.dot_general(
        query, keys, (((1,), (1,)), ((), ())), preferred_element_type=jnp.float32
    )
    scores = scores * SCALE
    if inside is not None:
        scores = jnp.where(inside, scores, -1e30)
    weights = jnp.exp(scores - jnp.max(scores, axis=1, keepdims=True))
    total = jnp.sum(weights, axis=1, keepdims=True)
    summed = jnp.dot(weights.astype(jnp.bfloat16), values, preferred_element_type=jnp.float32)
    return summed / total


def temporal_heads(low, frames, profile, window, query, key, value, *rest):
    arrived, rest = rest[: frames - 1], rest[frames - 1 :]
    outs, (near, apart, order, sems) = rest[:frames], rest[frames:]
    width = query.shape[1] // HD
    slots, chunk = outs[0].shape[0], outs[0].shape[1]
    mine = lax.axis_index("frame")
    total = list_heads(profile, order, 0, width)
    first = lax.axis_index("head") * width
    size = frames * chunk

    @pl.when(total > low)
    def _():
        rows = pl.ds(pl.multiple_of(mine * chunk, chunk), chunk)
        own = [
            pltpu.make_async_copy(source.at[rows], near.at[index], sems.at[index])
            for index, source in enumerate((query, key, value))
        ]
        for copy in own:
            copy.start()

        def place(dim):
            at = lax.broadcasted_iota(jnp.int32, (size, size), dim)
            frame = mine - at // chunk
            return jnp.where(frame < 0, frame + frames, frame), at % chunk

        (frame_row, token_row), (frame_col, token_col) = place(0), place(1)
        apart[...] = jnp.where(token_row == token_col, jnp.abs(frame_row - frame_col), frames + size)
        for copy in own:
            copy.wait()

        def one(slot, carry):
            head = order[low + slot]
            columns = columns_of(head)
            query_all, key_all, value_all = (
                jnp.concatenate([near[index, :, columns]] + [a[slot, index] for a in arrived])
                for index in range(3)
            )
            reach = jnp.minimum(window[first + head], frames)
            result = attend(query_all, key_all, value_all, apart[...] <= reach)
            for distance, out in enumerate(outs):
                out[slot] = result[distance * chunk : (distance + 1) * chunk].astype(out.dtype)
            return carry

        lax.fori_loop(0, slots, one, 0)


def put_back(lows, frames, profile, started, *rest):
    chunks = rest[: len(lows) * frames]
    out, order, sems = rest[len(lows) * frames :]
    width = out.shape[1] // HD
    mine = lax.axis_index("frame")
    total = list_heads(profile, order, 0, width)

    def copies():
        for group, low in enumerate(lows):
            for slot in range(chunks[group * frames].shape[0]):
                for distance in range(frames):
                    source = chunks[group * frames + distance]
                    chunk = source.shape[1]
                    at = lax.rem(mine + distance, frames)
                    rows = pl.ds(pl.multiple_of(at * chunk, chunk), chunk)
                    yield (
                        low + slot < total,
                        pltpu.make_async_copy(
                            source.at[slot],
                            out.at[rows, columns_of(order[low + slot])],
                            sems.at[(low + slot) * frames + distance],
                        ),
                    )

    for valid, copy in copies():

        @pl.when(valid)
        def _(copy=copy):
            copy.start()

    for valid, copy in copies():

        @pl.when(valid)
        def _(copy=copy):
            copy.wait()


def exchange(block, distance, only):
    frames, cores = lax.axis_size("frame"), lax.axis_size("head")
    senders = range(cores) if only is None else (only,)
    route = [
        (frame * cores + core, (frame + distance) % frames * cores + core)
        for frame in range(frames)
        for core in senders
    ]
    return lax.ppermute(block, ("frame", "head"), route)


def program(groups, spatial_slots, queries, key_states, value_states, profile, window):
    frames, spaces = lax.axis_size("frame"), lax.axis_size("space")
    rows, wide = queries.shape[0] * queries.shape[1], queries.shape[2]
    width, chunk = wide // HD, rows // frames
    query, key, value = (a.reshape(rows, wide) for a in (queries, key_states, value_states))
    kind = queries.dtype
    order = pltpu.SMEM((width,), jnp.int32)
    lows, low = [], 0
    for slots, _ in groups:
        lows.append(low)
        low += slots

    arrivals = []
    for (slots, only), low in zip(groups, lows):
        sends = pl.pallas_call(
            functools.partial(pack_chunks, low),
            out_shape=[jax.ShapeDtypeStruct((slots, 3, chunk, HD), kind)] * (frames - 1),
            in_specs=[SMALL, HBM, HBM, HBM],
            out_specs=[HBM] * (frames - 1),
            scratch_shapes=[order, pltpu.SemaphoreType.DMA((frames - 1,))],
            compiler_params=params(),
            cost_estimate=pl.CostEstimate(flops=0, bytes_accessed=slots * 6 * rows * HD * 2, transcendentals=0),
        )(profile, query, key, value)
        arrivals.append([exchange(block, distance, only) for distance, block in enumerate(sends, 1)])

    if spaces > 1:
        kept = pl.pallas_call(
            pack_rows,
            out_shape=jax.ShapeDtypeStruct((spatial_slots, 2, rows, HD), kind),
            in_specs=[SMALL, HBM, HBM],
            out_specs=HBM,
            scratch_shapes=[order, pltpu.SemaphoreType.DMA],
            compiler_params=params(),
            cost_estimate=pl.CostEstimate(flops=0, bytes_accessed=spatial_slots * 8 * rows * HD, transcendentals=0),
        )(profile, key, value)
        fetched = [
            lax.ppermute(kept, "space", [(i, (i + distance) % spaces) for i in range(spaces)])
            for distance in range(1, spaces)
        ]
    else:
        fetched = []
    started = pl.pallas_call(
        functools.partial(spatial_heads, spaces - 1),
        out_shape=jax.ShapeDtypeStruct((rows, wide), kind),
        in_specs=[SMALL] + [FAST] * (spaces + 2),
        out_specs=FAST,
        scratch_shapes=[order],
        compiler_params=params(),
        cost_estimate=pl.CostEstimate(
            flops=spatial_slots * 4 * rows * rows * spaces * HD,
            bytes_accessed=wide * rows * 16,
            transcendentals=spatial_slots * rows * rows * spaces,
        ),
    )(profile, query, key, value, *fetched)

    results = []
    for (slots, only), low, arrived in zip(groups, lows, arrivals):
        chunks = pl.pallas_call(
            functools.partial(temporal_heads, low, frames),
            out_shape=[jax.ShapeDtypeStruct((slots, chunk, HD), kind)] * frames,
            in_specs=[SMALL, SMALL] + [HBM] * 3 + [FAST] * (frames - 1),
            out_specs=[FAST] * frames,
            scratch_shapes=[
                pltpu.VMEM((3, chunk, wide), kind),
                pltpu.VMEM((rows, rows), jnp.int32),
                order,
                pltpu.SemaphoreType.DMA((3,)),
            ],
            compiler_params=params(),
            cost_estimate=pl.CostEstimate(
                flops=slots * 4 * rows * rows * HD,
                bytes_accessed=slots * rows * HD * 8,
                transcendentals=slots * rows * rows,
            ),
        )(profile, window, query, key, value, *arrived)
        results.append(chunks[0])
        results += [exchange(block, -distance, only) for distance, block in enumerate(chunks[1:], 1)]

    last = pl.pallas_call(
        functools.partial(put_back, lows, frames),
        out_shape=jax.ShapeDtypeStruct((rows, wide), kind),
        in_specs=[SMALL, HBM] + [HBM] * len(results),
        out_specs=HBM,
        scratch_shapes=[order, pltpu.SemaphoreType.DMA((width * frames,))],
        input_output_aliases={1: 0},
        compiler_params=params(),
        cost_estimate=pl.CostEstimate(flops=0, bytes_accessed=width * rows * HD * 2, transcendentals=0),
    )(profile, started, *results)
    return last.reshape(queries.shape)


def local(queries, key_states, value_states, profile, window):
    width = queries.shape[2] // HD
    half = width * lax.axis_size("head") // 2
    even = half // 2
    reach = 2
    first = jnp.sum((profile[:width] == 0).astype(jnp.int32))
    branches = []
    for extra in range(-reach, reach + 1):
        less, more = even - abs(extra), 2 * abs(extra)
        groups = [(less, None)] + ([(more, 0 if extra > 0 else 1)] if more else [])
        branches.append(functools.partial(program, groups, even + abs(extra)))
    branches.append(functools.partial(program, [(width, None)], width))
    offset = first - even + reach
    index = jnp.where((offset < 0) | (offset > 2 * reach), 2 * reach + 1, offset)
    return lax.switch(index, branches, queries, key_states, value_states, profile, window)


def solution(mesh):
    placed = P(("groups", "frame"), "space", "head")
    return jax.shard_map(
        local,
        mesh=mesh,
        in_specs=(placed, placed, placed, P(), P()),
        out_specs=placed,
        check_vma=False,
    )
```

```python
import functools

import jax
import jax.numpy as jnp
from jax import lax
from jax.experimental import pallas as pl
from jax.experimental.pallas import tpu as pltpu
from jax.sharding import PartitionSpec as P

HD = 128
HBM = pl.BlockSpec(memory_space=pl.ANY)
SMALL = pl.BlockSpec(memory_space=pltpu.SMEM)
FAST = pl.BlockSpec(memory_space=pltpu.VMEM)
SCALE = HD ** (-0.5)
AHEAD = 40 * 10**9


def list_heads(profile, order, kind, width):
    first = lax.axis_index("head") * width

    for i in range(width):
        order[i] = 0
    count = jnp.int32(0)
    for i in range(width):
        hit = profile[first + i] == kind

        @pl.when(hit)
        def _(i=i, count=count):
            order[count] = i

        count = count + hit.astype(jnp.int32)
    return count


def columns_of(head):
    return pl.ds(pl.multiple_of(head * HD, HD), HD)


def steps_of(frames):
    return [0] + sorted(range(1, frames), key=lambda step: step < frames // 2)


def partner(frame, step, frames):
    if frames & (frames - 1) == 0:
        return frame ^ step
    return (frame + step) % frames


def source_of(frame, step, frames):
    if frames & (frames - 1) == 0:
        return frame ^ step
    return (frame - step + frames) % frames


def params(megabytes=40):
    return pltpu.CompilerParams(vmem_limit_bytes=megabytes << 20)


def pack_chunks(profile, query, key, value, *rest):
    *sends, order, sems = rest
    frames = len(sends) + 1
    width = query.shape[1] // HD
    slots, chunk = sends[0].shape[0], sends[0].shape[2]
    mine = lax.axis_index("frame")
    list_heads(profile, order, 0, width)
    for distance, send in enumerate(sends, 1):
        to = partner(mine, steps_of(frames)[distance], frames)
        rows = pl.ds(pl.multiple_of(to * chunk, chunk), chunk)
        for slot in range(slots):
            columns = columns_of(order[slot])
            for index, source in enumerate((query, key, value)):
                pltpu.make_async_copy(
                    source.at[rows, columns], send.at[slot, index], sems.at[distance - 1]
                ).start()
    for distance, send in enumerate(sends, 1):
        pltpu.make_async_copy(send, send, sems.at[distance - 1]).wait()


def pack_rows(profile, key, value, after, send, order, sem):
    width = key.shape[1] // HD
    list_heads(profile, order, 1, width)

    for slot in range(send.shape[0]):
        columns = columns_of(order[slot])
        for index, source in enumerate((key, value)):
            pltpu.make_async_copy(source.at[:, columns], send.at[slot, index], sem).start()
    pltpu.make_async_copy(send, send, sem).wait()


def spatial_heads(size, peers, profile, query, key, value, *rest):
    fetched, (out, order) = rest[:peers], rest[peers:]
    width = query.shape[1] // HD
    list_heads(profile, order, 1, width)

    def one(slot, carry):
        columns = columns_of(order[slot])
        keys = jnp.concatenate([key[:, columns]] + [f[slot, 0] for f in fetched])
        values = jnp.concatenate([value[:, columns]] + [f[slot, 1] for f in fetched])
        weights, whole = soften(score(query[:, columns], keys))
        out[:, columns] = blend(weights, whole, values).astype(out.dtype)
        return carry

    lax.fori_loop(0, size, one, 0)


def score(query, keys):
    return SCALE * lax.dot_general(
        query, keys, (((1,), (1,)), ((), ())), preferred_element_type=jnp.float32
    )


def soften(scores):
    weights = jnp.exp(scores - jnp.max(scores, axis=1, keepdims=True))
    return weights.astype(jnp.bfloat16), jnp.sum(weights, axis=1, keepdims=True)


def blend(weights, total, values):
    return jnp.dot(weights, values, preferred_element_type=jnp.float32) / total


def temporal_heads(frames, profile, window, query, key, value, *rest):
    arrived, rest = rest[: frames - 1], rest[frames - 1 :]
    outs, (near, apart, order, sems) = rest[:frames], rest[frames:]
    width = query.shape[1] // HD
    slots, chunk = outs[0].shape[0], outs[0].shape[1]
    mine = lax.axis_index("frame")
    list_heads(profile, order, 0, width)
    first = lax.axis_index("head") * width
    part = apart.shape[0] // frames
    size = frames * part

    rows = pl.ds(pl.multiple_of(mine * chunk, chunk), chunk)
    own = [
        pltpu.make_async_copy(source.at[rows], near.at[index], sems.at[index])
        for index, source in enumerate((query, key, value))
    ]
    for copy in own:
        copy.start()

    def place(dim):
        at = lax.broadcasted_iota(jnp.int32, (size, size), dim)
        steps = steps_of(frames)
        passed = [(at >= i * part).astype(jnp.int32) for i in range(1, frames)]
        step = sum(p * (steps[i] - steps[i - 1]) for i, p in enumerate(passed, 1))
        return source_of(mine, step, frames), at - sum(passed) * part

    (frame_row, token_row), (frame_col, token_col) = place(0), place(1)
    apart[...] = jnp.where(token_row == token_col, jnp.abs(frame_row - frame_col), frames + size)
    for copy in own:
        copy.wait()

    def several(slots):
        pieces, scores = [], []
        for slot in slots:
            head = order[slot]
            columns = columns_of(head)
            inside = apart[...] <= jnp.minimum(window[first + head], frames)
            for start in range(0, chunk, part):
                tokens = slice(start, start + part)
                query_all, key_all, value_all = (
                    jnp.concatenate([near[index, tokens, columns]] + [a[slot, index, tokens] for a in arrived])
                    for index in range(3)
                )
                pieces.append((slot, tokens, value_all))
                scores.append(jnp.where(inside, score(query_all, key_all), -1e30))
        weights = [soften(one) for one in scores]
        for (slot, tokens, value_all), (weight, total) in zip(pieces, weights):
            result = blend(weight, total, value_all).astype(outs[0].dtype)
            for distance, out in enumerate(outs):
                out[slot, tokens] = result[distance * part : (distance + 1) * part]

    if slots <= 9:
        several(range(slots))
    else:

        def one(slot, carry):
            several([slot])
            return carry

        lax.fori_loop(0, slots, one, 0)


def put_back(sure, frames, profile, *rest):
    chunks = rest[:frames]
    _, out, order, sems = rest[frames:]
    width = out.shape[1] // HD
    mine = lax.axis_index("frame")
    total = list_heads(profile, order, 0, width)
    slots, chunk = chunks[0].shape[0], chunks[0].shape[1]

    def copies(slot):
        for distance, source in enumerate(chunks):
            at = partner(mine, steps_of(frames)[distance], frames)
            rows = pl.ds(pl.multiple_of(at * chunk, chunk), chunk)
            sem = sems.at[distance if slot < sure else slot * frames + distance]
            yield pltpu.make_async_copy(source.at[slot], out.at[rows, columns_of(order[slot])], sem)

    for slot in range(sure):
        for copy in copies(slot):
            copy.start()
    for slot in range(sure, slots):

        @pl.when(slot < total)
        def _(slot=slot):
            for copy in copies(slot):
                copy.start()

    if sure:
        for distance, source in enumerate(chunks):
            part = source.at[:sure]
            pltpu.make_async_copy(part, part, sems.at[distance]).wait()
    for slot in range(sure, slots):

        @pl.when(slot < total)
        def _(slot=slot):
            for copy in copies(slot):
                copy.wait()


def exchange(block, index, back=False):
    frames = lax.axis_size("frame")
    step = steps_of(frames)[index]
    route = [(frame, partner(frame, step, frames)) for frame in range(frames)]
    return lax.ppermute(block, "frame", [(b, a) for a, b in route] if back else route)


def program(size, queries, key_states, value_states, profile, window):
    frames, spaces = lax.axis_size("frame"), lax.axis_size("space")
    rows, wide = queries.shape[0] * queries.shape[1], queries.shape[2]
    width, chunk = wide // HD, rows // frames
    part = chunk // 2 if chunk % 32 == 0 else chunk
    query, key, value = (a.reshape(rows, wide) for a in (queries, key_states, value_states))
    kind = queries.dtype
    order = pltpu.SMEM((width,), jnp.int32)
    sure = width * lax.axis_size("head") // 2 - size
    sends = pl.pallas_call(
        pack_chunks,
        out_shape=[jax.ShapeDtypeStruct((size, 3, chunk, HD), kind)] * (frames - 1),
        in_specs=[SMALL, HBM, HBM, HBM],
        out_specs=[HBM] * (frames - 1),
        scratch_shapes=[order, pltpu.SemaphoreType.DMA((frames - 1,))],
        compiler_params=params(),
        cost_estimate=pl.CostEstimate(flops=0, bytes_accessed=size * rows * HD * 12, transcendentals=0),
    )(profile, query, key, value)
    arrived = [exchange(block, index) for index, block in enumerate(sends, 1)]

    if spaces > 1:
        kept = pl.pallas_call(
            pack_rows,
            out_shape=jax.ShapeDtypeStruct((size, 2, rows, HD), kind),
            in_specs=[SMALL, HBM, HBM, HBM],
            out_specs=HBM,
            scratch_shapes=[order, pltpu.SemaphoreType.DMA],
            compiler_params=params(),
            cost_estimate=pl.CostEstimate(flops=0, bytes_accessed=size * 8 * rows * HD, transcendentals=0),
        )(profile, key, value, sends[-1])
        fetched = [
            lax.ppermute(kept, "space", [(i, (i + distance) % spaces) for i in range(spaces)])
            for distance in range(1, spaces)
        ]
    else:
        fetched = []
    started = pl.pallas_call(
        functools.partial(spatial_heads, size, spaces - 1),
        out_shape=jax.ShapeDtypeStruct((rows, wide), kind),
        in_specs=[SMALL] + [FAST] * (spaces + 2),
        out_specs=FAST,
        scratch_shapes=[order],
        compiler_params=params(),
        cost_estimate=pl.CostEstimate(
            flops=size * 4 * rows * rows * spaces * HD,
            bytes_accessed=wide * rows * 16,
            transcendentals=size * rows * rows * spaces,
        ),
    )(profile, query, key, value, *fetched)

    chunks = pl.pallas_call(
        functools.partial(temporal_heads, frames),
        out_shape=[jax.ShapeDtypeStruct((size, chunk, HD), kind)] * frames,
        in_specs=[SMALL, SMALL] + [HBM] * 3 + [FAST] * (frames - 1),
        out_specs=[FAST] * frames,
        scratch_shapes=[
            pltpu.VMEM((3, chunk, wide), kind),
            pltpu.VMEM((frames * part, frames * part), jnp.int32),
            order,
            pltpu.SemaphoreType.DMA((3,)),
        ],
        compiler_params=params(),
        cost_estimate=pl.CostEstimate(
            flops=AHEAD,
            bytes_accessed=size * rows * HD * 8,
            transcendentals=size * rows * rows,
        ),
    )(profile, window, query, key, value, *arrived)
    results = [chunks[0]] + [exchange(block, index, True) for index, block in enumerate(chunks[1:], 1)]

    last = pl.pallas_call(
        functools.partial(put_back, sure, frames),
        out_shape=jax.ShapeDtypeStruct((rows, wide), kind),
        in_specs=[SMALL] + [HBM] * (len(results) + 1),
        out_specs=HBM,
        scratch_shapes=[order, pltpu.SemaphoreType.DMA(((width + 1) * frames,))],
        input_output_aliases={len(results) + 1: 0},
        compiler_params=params(),
        cost_estimate=pl.CostEstimate(flops=0, bytes_accessed=width * rows * HD * 2, transcendentals=0),
    )(profile, *results, started)
    return last.reshape(queries.shape)


def local(queries, key_states, value_states, profile, window):
    width = queries.shape[2] // HD
    half = width * lax.axis_size("head") // 2
    even = half // 2
    first = jnp.sum((profile[:width] == 0).astype(jnp.int32))
    sizes = sorted({min(even + more, width) for more in (0, 1, 2, 3)} | {width})
    branches = [functools.partial(program, size) for size in sizes]
    larger = jnp.maximum(first, half - first)
    index = sum((larger > size).astype(jnp.int32) for size in sizes[:-1])
    return lax.switch(index, branches, queries, key_states, value_states, profile, window)


def solution(mesh):
    placed = P(("groups", "frame"), "space", "head")
    return jax.shard_map(
        local,
        mesh=mesh,
        in_specs=(placed, placed, placed, P(), P()),
        out_specs=placed,
        check_vma=False,
    )
```

```python
import functools

import jax
import jax.numpy as jnp
from jax import lax
from jax.experimental import pallas as pl
from jax.experimental.pallas import tpu as pltpu
from jax.sharding import PartitionSpec as P

HD = 128
HBM = pl.BlockSpec(memory_space=pl.ANY)
SMALL = pl.BlockSpec(memory_space=pltpu.SMEM)
FAST = pl.BlockSpec(memory_space=pltpu.VMEM)
SCALE = HD ** (-0.5)
AHEAD = 40 * 10**9


def list_heads(profile, order, kind, width):
    first = lax.axis_index("head") * width

    for i in range(width):
        order[i] = 0
    count = jnp.int32(0)
    for i in range(width):
        hit = profile[first + i] == kind

        @pl.when(hit)
        def _(i=i, count=count):
            order[count] = i

        count = count + hit.astype(jnp.int32)
    return count


def columns_of(head):
    return pl.ds(pl.multiple_of(head * HD, HD), HD)


def steps_of(frames):
    return [0] + list(range(frames - 1, 0, -1))


def long_steps(frames):
    return [step for step in steps_of(frames) if step and (step >= frames // 2 or frames & (frames - 1))]


def partner(frame, step, frames):
    if frames & (frames - 1) == 0:
        return frame ^ step
    return (frame + step) % frames


def source_of(frame, step, frames):
    if frames & (frames - 1) == 0:
        return frame ^ step
    return (frame - step + frames) % frames


def params(megabytes=40):
    return pltpu.CompilerParams(vmem_limit_bytes=megabytes << 20)


def pack_chunks(low, steps, profile, query, key, value, after, *rest):
    sends, (order, sems) = rest[: len(steps)], rest[len(steps) :]
    list_heads(profile, order, 0, query.shape[1] // HD)
    frames, mine = lax.axis_size("frame"), lax.axis_index("frame")
    for number, (step, send) in enumerate(zip(steps, sends)):
        slots, chunk = send.shape[0], send.shape[2]
        rows = pl.ds(pl.multiple_of(partner(mine, step, frames) * chunk, chunk), chunk)
        for slot in range(slots):
            columns = columns_of(order[low + slot])
            for index, source in enumerate((query, key, value)):
                pltpu.make_async_copy(source.at[rows, columns], send.at[slot, index], sems.at[number]).start()
    for number, send in enumerate(sends):
        pltpu.make_async_copy(send, send, sems.at[number]).wait()


def pack_rows(profile, key, value, after, send, order, sem):
    width = key.shape[1] // HD
    list_heads(profile, order, 1, width)

    for slot in range(send.shape[0]):
        columns = columns_of(order[slot])
        for index, source in enumerate((key, value)):
            pltpu.make_async_copy(source.at[:, columns], send.at[slot, index], sem).start()
    pltpu.make_async_copy(send, send, sem).wait()


def spatial_heads(size, peers, profile, query, key, value, *rest):
    fetched, (out, order) = rest[:peers], rest[peers:]
    width = query.shape[1] // HD
    list_heads(profile, order, 1, width)

    def one(slot, carry):
        columns = columns_of(order[slot])
        keys = jnp.concatenate([key[:, columns]] + [f[slot, 0] for f in fetched])
        values = jnp.concatenate([value[:, columns]] + [f[slot, 1] for f in fetched])
        weights, whole = soften(score(query[:, columns], keys))
        out[:, columns] = blend(weights, whole, values).astype(out.dtype)
        return carry

    lax.fori_loop(0, size, one, 0)


def score(query, keys):
    return SCALE * lax.dot_general(
        query, keys, (((1,), (1,)), ((), ())), preferred_element_type=jnp.float32
    )


def soften(scores):
    weights = jnp.exp(scores - jnp.max(scores, axis=1, keepdims=True))
    return weights.astype(jnp.bfloat16), jnp.sum(weights, axis=1, keepdims=True)


def blend(weights, total, values):
    return jnp.dot(weights, values, preferred_element_type=jnp.float32) / total


def temporal_heads(frames, extras, profile, window, query, key, value, *rest):
    arrived, rest = rest[: frames - 1], rest[frames - 1 :]
    extra, rest = rest[:extras], rest[extras:]
    outs, (near, apart, order, sems) = rest[:frames], rest[frames:]
    width = query.shape[1] // HD
    slots, chunk = outs[0].shape[0], outs[0].shape[1]
    mine = lax.axis_index("frame")
    list_heads(profile, order, 0, width)
    first = lax.axis_index("head") * width
    part = apart.shape[0] // frames
    size = frames * part

    rows = pl.ds(pl.multiple_of(mine * chunk, chunk), chunk)
    own = [
        pltpu.make_async_copy(source.at[rows], near.at[index], sems.at[index])
        for index, source in enumerate((query, key, value))
    ]
    for copy in own:
        copy.start()

    def place(dim):
        at = lax.broadcasted_iota(jnp.int32, (size, size), dim)
        steps = steps_of(frames)
        passed = [(at >= i * part).astype(jnp.int32) for i in range(1, frames)]
        step = sum(p * (steps[i] - steps[i - 1]) for i, p in enumerate(passed, 1))
        return source_of(mine, step, frames), at - sum(passed) * part

    (frame_row, token_row), (frame_col, token_col) = place(0), place(1)
    apart[...] = jnp.where(token_row == token_col, jnp.abs(frame_row - frame_col), frames + size)
    for copy in own:
        copy.wait()

    def chunk_of(number, slot, index, tokens):
        common = arrived[number]
        if isinstance(slot, int) and slot >= common.shape[0]:
            return extra[number][slot - common.shape[0], index, tokens]
        return common[slot, index, tokens]

    def several(slots):
        pieces, scores = [], []
        for slot in slots:
            head = order[slot]
            columns = columns_of(head)
            inside = apart[...] <= jnp.minimum(window[first + head], frames)
            for start in range(0, chunk, part):
                tokens = slice(start, start + part)
                query_all, key_all, value_all = (
                    jnp.concatenate(
                        [near[index, tokens, columns]]
                        + [chunk_of(number, slot, index, tokens) for number in range(frames - 1)]
                    )
                    for index in range(3)
                )
                pieces.append((slot, tokens, value_all))
                scores.append(jnp.where(inside, score(query_all, key_all), -1e30))
        weights = [soften(one) for one in scores]
        for (slot, tokens, value_all), (weight, total) in zip(pieces, weights):
            result = blend(weight, total, value_all).astype(outs[0].dtype)
            for distance, out in enumerate(outs):
                out[slot, tokens] = result[distance * part : (distance + 1) * part]

    if slots <= 9:
        several(range(slots))
    else:

        def one(slot, carry):
            several([slot])
            return carry

        lax.fori_loop(0, slots, one, 0)


def put_back(sure, frames, profile, *rest):
    chunks = rest[:frames]
    _, out, order, sems = rest[frames:]
    width = out.shape[1] // HD
    mine = lax.axis_index("frame")
    total = list_heads(profile, order, 0, width)
    slots, chunk = chunks[0].shape[0], chunks[0].shape[1]

    def copies(slot):
        for distance, source in enumerate(chunks):
            at = partner(mine, steps_of(frames)[distance], frames)
            rows = pl.ds(pl.multiple_of(at * chunk, chunk), chunk)
            sem = sems.at[distance if slot < sure else slot * frames + distance]
            yield pltpu.make_async_copy(source.at[slot], out.at[rows, columns_of(order[slot])], sem)

    for slot in range(sure):
        for copy in copies(slot):
            copy.start()
    for slot in range(sure, slots):

        @pl.when(slot < total)
        def _(slot=slot):
            for copy in copies(slot):
                copy.start()

    if sure:
        for distance, source in enumerate(chunks):
            part = source.at[:sure]
            pltpu.make_async_copy(part, part, sems.at[distance]).wait()
    for slot in range(sure, slots):

        @pl.when(slot < total)
        def _(slot=slot):
            for copy in copies(slot):
                copy.wait()


def exchange(block, step, back=False, only=None):
    frames, cores = lax.axis_size("frame"), lax.axis_size("head")
    route = []
    for frame in range(frames):
        ends = (frame, partner(frame, step, frames))
        source, target = ends[::-1] if back else ends
        route += [(source * cores + core, target * cores + core) for core in range(cores) if only in (None, core)]
    return lax.ppermute(block, ("frame", "head"), route)


def program(size, rich, queries, key_states, value_states, profile, window):
    frames, spaces = lax.axis_size("frame"), lax.axis_size("space")
    rows, wide = queries.shape[0] * queries.shape[1], queries.shape[2]
    width, chunk = wide // HD, rows // frames
    part = chunk // 2 if chunk % 32 == 0 else chunk
    query, key, value = (a.reshape(rows, wide) for a in (queries, key_states, value_states))
    kind = queries.dtype
    order = pltpu.SMEM((width,), jnp.int32)
    sure = width * lax.axis_size("head") // 2 - size
    steps, far = steps_of(frames)[1:], long_steps(frames)
    common = size if rich is None else sure

    def pack(low, steps, counts, after):
        return pl.pallas_call(
            functools.partial(pack_chunks, low, steps),
            out_shape=[jax.ShapeDtypeStruct((count, 3, chunk, HD), kind) for count in counts],
            in_specs=[SMALL] + [HBM] * 4,
            out_specs=[HBM] * len(steps),
            scratch_shapes=[order, pltpu.SemaphoreType.DMA((len(steps),))],
            compiler_params=params(),
            cost_estimate=pl.CostEstimate(flops=0, bytes_accessed=sum(counts) * chunk * HD * 12, transcendentals=0),
        )(profile, query, key, value, after)

    sends = pack(0, steps, [common if step in far else size for step in steps], query)
    arrived = [exchange(block, step) for step, block in zip(steps, sends)]
    after = sends[-1]

    if spaces > 1:
        kept = pl.pallas_call(
            pack_rows,
            out_shape=jax.ShapeDtypeStruct((size, 2, rows, HD), kind),
            in_specs=[SMALL, HBM, HBM, HBM],
            out_specs=HBM,
            scratch_shapes=[order, pltpu.SemaphoreType.DMA],
            compiler_params=params(),
            cost_estimate=pl.CostEstimate(flops=0, bytes_accessed=size * 8 * rows * HD, transcendentals=0),
        )(profile, key, value, after)
        fetched = [
            lax.ppermute(kept, "space", [(i, (i + distance) % spaces) for i in range(spaces)])
            for distance in range(1, spaces)
        ]
        after = kept
    else:
        fetched = []
    extra = []
    if common < size:
        sends = pack(common, far, [size - common] * len(far), after)
        extra = [exchange(block, step, only=rich) for step, block in zip(far, sends)]
    started = pl.pallas_call(
        functools.partial(spatial_heads, size, spaces - 1),
        out_shape=jax.ShapeDtypeStruct((rows, wide), kind),
        in_specs=[SMALL] + [FAST] * (spaces + 2),
        out_specs=FAST,
        scratch_shapes=[order],
        compiler_params=params(),
        cost_estimate=pl.CostEstimate(
            flops=size * 4 * rows * rows * spaces * HD,
            bytes_accessed=wide * rows * 16,
            transcendentals=size * rows * rows * spaces,
        ),
    )(profile, query, key, value, *fetched)

    chunks = pl.pallas_call(
        functools.partial(temporal_heads, frames, len(extra)),
        out_shape=[jax.ShapeDtypeStruct((size, chunk, HD), kind)] * frames,
        in_specs=[SMALL, SMALL] + [HBM] * 3 + [FAST] * (frames - 1 + len(extra)),
        out_specs=[FAST] * frames,
        scratch_shapes=[
            pltpu.VMEM((3, chunk, wide), kind),
            pltpu.VMEM((frames * part, frames * part), jnp.int32),
            order,
            pltpu.SemaphoreType.DMA((3,)),
        ],
        compiler_params=params(),
        cost_estimate=pl.CostEstimate(
            flops=AHEAD,
            bytes_accessed=size * rows * HD * 8,
            transcendentals=size * rows * rows,
        ),
    )(profile, window, query, key, value, *arrived, *extra)
    results = [chunks[0]] + [exchange(block, step, back=True) for step, block in zip(steps, chunks[1:])]

    last = pl.pallas_call(
        functools.partial(put_back, sure, frames),
        out_shape=jax.ShapeDtypeStruct((rows, wide), kind),
        in_specs=[SMALL] + [HBM] * (len(results) + 1),
        out_specs=HBM,
        scratch_shapes=[order, pltpu.SemaphoreType.DMA(((width + 1) * frames,))],
        input_output_aliases={len(results) + 1: 0},
        compiler_params=params(),
        cost_estimate=pl.CostEstimate(flops=0, bytes_accessed=width * rows * HD * 2, transcendentals=0),
    )(profile, *results, started)
    return last.reshape(queries.shape)


def local(queries, key_states, value_states, profile, window):
    width = queries.shape[2] // HD
    half = width * lax.axis_size("head") // 2
    even = half // 2
    first = jnp.sum((profile[:width] == 0).astype(jnp.int32))
    reach = min(3, even)
    branches = [
        functools.partial(program, even + abs(more), None if more == 0 else int(more < 0))
        for more in range(-reach, reach + 1)
    ]
    branches.append(functools.partial(program, width, None))
    offset = first - even + reach
    index = jnp.where((offset < 0) | (offset > 2 * reach), 2 * reach + 1, offset)
    return lax.switch(index, branches, queries, key_states, value_states, profile, window)


def solution(mesh):
    placed = P(("groups", "frame"), "space", "head")
    return jax.shard_map(
        local,
        mesh=mesh,
        in_specs=(placed, placed, placed, P(), P()),
        out_specs=placed,
        check_vma=False,
    )
```

```python
import functools

import jax
import jax.numpy as jnp
from jax import lax
from jax.experimental import pallas as pl
from jax.experimental.pallas import tpu as pltpu
from jax.sharding import PartitionSpec as P

HD = 128
HBM = pl.BlockSpec(memory_space=pl.ANY)
SMALL = pl.BlockSpec(memory_space=pltpu.SMEM)
FAST = pl.BlockSpec(memory_space=pltpu.VMEM)
SCALE = HD ** (-0.5)
AHEAD = 7 * 10**9


def list_heads(profile, order, kind, width):
    first = lax.axis_index("head") * width

    for i in range(width):
        order[i] = 0
    count = jnp.int32(0)
    for i in range(width):
        hit = profile[first + i] == kind

        @pl.when(hit)
        def _(i=i, count=count):
            order[count] = i

        count = count + hit.astype(jnp.int32)
    return count


def columns_of(head):
    return pl.ds(pl.multiple_of(head * HD, HD), HD)


def steps_of(frames):
    return [0] + list(range(frames - 1, 0, -1))


def long_steps(frames, surplus):
    least = 3 * frames if surplus <= 2 else 2 * frames
    return [step for step in steps_of(frames) if step and 4 * step >= least]


def partner(frame, step, frames):
    if frames & (frames - 1) == 0:
        return frame ^ step
    return (frame + step) % frames


def source_of(frame, step, frames):
    if frames & (frames - 1) == 0:
        return frame ^ step
    return (frame - step + frames) % frames


def params(megabytes=40):
    return pltpu.CompilerParams(vmem_limit_bytes=megabytes << 20)


def pack_chunks(low, steps, profile, query, key, value, after, *rest):
    sends, (order, sems) = rest[: len(steps)], rest[len(steps) :]
    list_heads(profile, order, 0, query.shape[1] // HD)
    frames, mine = lax.axis_size("frame"), lax.axis_index("frame")
    for number, (step, send) in enumerate(zip(steps, sends)):
        slots, chunk = send.shape[0], send.shape[2]
        rows = pl.ds(pl.multiple_of(partner(mine, step, frames) * chunk, chunk), chunk)
        for slot in range(slots):
            columns = columns_of(order[low + slot])
            for index, source in enumerate((query, key, value)):
                pltpu.make_async_copy(source.at[rows, columns], send.at[slot, index], sems.at[number]).start()
    for number, send in enumerate(sends):
        pltpu.make_async_copy(send, send, sems.at[number]).wait()


def prepare(frames, profile, query, key, value, after, send, near, apart, order, sems):
    width = key.shape[1] // HD
    mine = lax.axis_index("frame")
    slots, _, chunk, _ = near.shape
    list_heads(profile, order, 1, width)
    for slot in range(send.shape[0]):
        columns = columns_of(order[slot])
        for index, source in enumerate((key, value)):
            pltpu.make_async_copy(source.at[:, columns], send.at[slot, index], sems.at[0]).start()
    list_heads(profile, order, 0, width)
    rows = pl.ds(pl.multiple_of(mine * chunk, chunk), chunk)
    for slot in range(slots):
        columns = columns_of(order[slot])
        for index, source in enumerate((query, key, value)):
            pltpu.make_async_copy(source.at[rows, columns], near.at[slot, index], sems.at[1]).start()

    size = apart.shape[0]
    part = size // frames
    steps = steps_of(frames)

    def place(dim):
        at = lax.broadcasted_iota(jnp.int32, (size, size), dim)
        passed = [(at >= i * part).astype(jnp.int32) for i in range(1, frames)]
        step = sum(p * (steps[i] - steps[i - 1]) for i, p in enumerate(passed, 1))
        return source_of(mine, step, frames), at - sum(passed) * part

    (frame_row, token_row), (frame_col, token_col) = place(0), place(1)
    apart[...] = jnp.where(token_row == token_col, jnp.abs(frame_row - frame_col), frames + size)
    pltpu.make_async_copy(send, send, sems.at[0]).wait()
    pltpu.make_async_copy(near, near, sems.at[1]).wait()


def spatial_heads(size, peers, profile, query, key, value, *rest):
    fetched, (out, order) = rest[:peers], rest[peers:]
    width = query.shape[1] // HD
    list_heads(profile, order, 1, width)

    def one(slot, carry):
        columns = columns_of(order[slot])
        keys = jnp.concatenate([key[:, columns]] + [f[slot, 0] for f in fetched])
        values = jnp.concatenate([value[:, columns]] + [f[slot, 1] for f in fetched])
        weights, whole = soften(score(query[:, columns], keys))
        out[:, columns] = blend(weights, whole, values).astype(out.dtype)
        return carry

    lax.fori_loop(0, size, one, 0)


def score(query, keys):
    return SCALE * lax.dot_general(
        query, keys, (((1,), (1,)), ((), ())), preferred_element_type=jnp.float32
    )


def soften(scores):
    weights = jnp.exp(scores - jnp.max(scores, axis=1, keepdims=True))
    return weights.astype(jnp.bfloat16), jnp.sum(weights, axis=1, keepdims=True)


def blend(weights, total, values):
    return jnp.dot(weights, values, preferred_element_type=jnp.float32) / total


def temporal_heads(frames, extras, profile, window, near, apart, *rest):
    arrived, rest = rest[: frames - 1], rest[frames - 1 :]
    extra, rest = rest[:extras], rest[extras:]
    outs, order = rest[:frames], rest[frames]
    width = profile.shape[0] // lax.axis_size("head")
    slots, chunk = outs[0].shape[0], outs[0].shape[1]
    list_heads(profile, order, 0, width)
    first = lax.axis_index("head") * width
    part = apart.shape[0] // frames

    def chunk_of(number, slot, index, tokens):
        common = arrived[number]
        if isinstance(slot, int) and slot >= common.shape[0]:
            return extra[number][slot - common.shape[0], index, tokens]
        return common[slot, index, tokens]

    def several(slots):
        pieces, scores = [], []
        for slot in slots:
            inside = apart[...] <= jnp.minimum(window[first + order[slot]], frames)
            for start in range(0, chunk, part):
                tokens = slice(start, start + part)
                query_all, key_all, value_all = (
                    jnp.concatenate(
                        [near[slot, index, tokens]]
                        + [chunk_of(number, slot, index, tokens) for number in range(frames - 1)]
                    )
                    for index in range(3)
                )
                pieces.append((slot, tokens, value_all))
                scores.append(jnp.where(inside, score(query_all, key_all), -1e30))
        weights = [soften(one) for one in scores]
        for (slot, tokens, value_all), (weight, total) in zip(pieces, weights):
            result = blend(weight, total, value_all).astype(outs[0].dtype)
            for distance, out in enumerate(outs):
                out[slot, tokens] = result[distance * part : (distance + 1) * part]

    if slots <= 9:
        several(range(slots))
    else:

        def one(slot, carry):
            several([slot])
            return carry

        lax.fori_loop(0, slots, one, 0)


def put_back(sure, frames, profile, *rest):
    chunks = rest[:frames]
    _, out, order, sems = rest[frames:]
    width = out.shape[1] // HD
    mine = lax.axis_index("frame")
    total = list_heads(profile, order, 0, width)
    slots, chunk = chunks[0].shape[0], chunks[0].shape[1]

    def copies(slot):
        for distance, source in enumerate(chunks):
            at = partner(mine, steps_of(frames)[distance], frames)
            rows = pl.ds(pl.multiple_of(at * chunk, chunk), chunk)
            sem = sems.at[distance if slot < sure else slot * frames + distance]
            yield pltpu.make_async_copy(source.at[slot], out.at[rows, columns_of(order[slot])], sem)

    for slot in range(sure):
        for copy in copies(slot):
            copy.start()
    for slot in range(sure, slots):

        @pl.when(slot < total)
        def _(slot=slot):
            for copy in copies(slot):
                copy.start()

    if sure:
        for distance, source in enumerate(chunks):
            part = source.at[:sure]
            pltpu.make_async_copy(part, part, sems.at[distance]).wait()
    for slot in range(sure, slots):

        @pl.when(slot < total)
        def _(slot=slot):
            for copy in copies(slot):
                copy.wait()


def exchange(block, step, back=False, only=None):
    frames, cores = lax.axis_size("frame"), lax.axis_size("head")
    route = []
    for frame in range(frames):
        ends = (frame, partner(frame, step, frames))
        source, target = ends[::-1] if back else ends
        route += [(source * cores + core, target * cores + core) for core in range(cores) if only in (None, core)]
    return lax.ppermute(block, ("frame", "head"), route)


def program(size, rich, queries, key_states, value_states, profile, window):
    frames, spaces = lax.axis_size("frame"), lax.axis_size("space")
    rows, wide = queries.shape[0] * queries.shape[1], queries.shape[2]
    width, chunk = wide // HD, rows // frames
    part = chunk // 2 if chunk % 32 == 0 else chunk
    query, key, value = (a.reshape(rows, wide) for a in (queries, key_states, value_states))
    kind = queries.dtype
    order = pltpu.SMEM((width,), jnp.int32)
    sure = width * lax.axis_size("head") // 2 - size
    steps = steps_of(frames)[1:]
    common = size if rich is None else sure
    far = long_steps(frames, size - common)

    def pack(low, steps, counts, after):
        return pl.pallas_call(
            functools.partial(pack_chunks, low, steps),
            out_shape=[jax.ShapeDtypeStruct((count, 3, chunk, HD), kind) for count in counts],
            in_specs=[SMALL] + [HBM] * 4,
            out_specs=[HBM] * len(steps),
            scratch_shapes=[order, pltpu.SemaphoreType.DMA((len(steps),))],
            compiler_params=params(),
            cost_estimate=pl.CostEstimate(flops=0, bytes_accessed=sum(counts) * chunk * HD * 12, transcendentals=0),
        )(profile, query, key, value, after)

    sends = pack(0, steps, [common if step in far else size for step in steps], query)
    arrived = [exchange(block, step) for step, block in zip(steps, sends)]

    kept, near, apart = pl.pallas_call(
        functools.partial(prepare, frames),
        out_shape=[
            jax.ShapeDtypeStruct((size, 2, rows, HD), kind),
            jax.ShapeDtypeStruct((size, 3, chunk, HD), kind),
            jax.ShapeDtypeStruct((frames * part, frames * part), jnp.int32),
        ],
        in_specs=[SMALL] + [HBM] * 4,
        out_specs=[HBM, HBM, FAST],
        scratch_shapes=[order, pltpu.SemaphoreType.DMA((2,))],
        compiler_params=params(),
        cost_estimate=pl.CostEstimate(flops=0, bytes_accessed=size * 16 * rows * HD, transcendentals=0),
    )(profile, query, key, value, sends[-1])
    fetched = [
        lax.ppermute(kept, "space", [(i, (i + distance) % spaces) for i in range(spaces)])
        for distance in range(1, spaces)
    ]
    extra = []
    if common < size:
        sends = pack(common, far, [size - common] * len(far), kept)
        extra = [exchange(block, step, only=rich) for step, block in zip(far, sends)]
    started = pl.pallas_call(
        functools.partial(spatial_heads, size, spaces - 1),
        out_shape=jax.ShapeDtypeStruct((rows, wide), kind),
        in_specs=[SMALL] + [FAST] * (spaces + 2),
        out_specs=FAST,
        scratch_shapes=[order],
        compiler_params=params(),
        cost_estimate=pl.CostEstimate(
            flops=size * 4 * rows * rows * spaces * HD,
            bytes_accessed=wide * rows * 16,
            transcendentals=size * rows * rows * spaces,
        ),
    )(profile, query, key, value, *fetched)

    chunks = pl.pallas_call(
        functools.partial(temporal_heads, frames, len(extra)),
        out_shape=[jax.ShapeDtypeStruct((size, chunk, HD), kind)] * frames,
        in_specs=[SMALL, SMALL] + [FAST] * (frames + 1 + len(extra)),
        out_specs=[FAST] * frames,
        scratch_shapes=[order],
        compiler_params=params(),
        cost_estimate=pl.CostEstimate(
            flops=AHEAD,
            bytes_accessed=size * rows * HD * 8,
            transcendentals=size * rows * rows,
        ),
    )(profile, window, near, apart, *arrived, *extra)
    results = [chunks[0]] + [exchange(block, step, back=True) for step, block in zip(steps, chunks[1:])]

    last = pl.pallas_call(
        functools.partial(put_back, sure, frames),
        out_shape=jax.ShapeDtypeStruct((rows, wide), kind),
        in_specs=[SMALL] + [HBM] * (len(results) + 1),
        out_specs=HBM,
        scratch_shapes=[order, pltpu.SemaphoreType.DMA(((width + 1) * frames,))],
        input_output_aliases={len(results) + 1: 0},
        compiler_params=params(),
        cost_estimate=pl.CostEstimate(flops=0, bytes_accessed=width * rows * HD * 2, transcendentals=0),
    )(profile, *results, started)
    return last.reshape(queries.shape)


def local(queries, key_states, value_states, profile, window):
    width = queries.shape[2] // HD
    half = width * lax.axis_size("head") // 2
    even = half // 2
    first = jnp.sum((profile[:width] == 0).astype(jnp.int32))
    reach = min(3, even)
    branches = [
        functools.partial(program, even + abs(more), None if more == 0 else int(more < 0))
        for more in range(-reach, reach + 1)
    ]
    branches.append(functools.partial(program, width, None))
    offset = first - even + reach
    index = jnp.where((offset < 0) | (offset > 2 * reach), 2 * reach + 1, offset)
    return lax.switch(index, branches, queries, key_states, value_states, profile, window)


def solution(mesh):
    placed = P(("groups", "frame"), "space", "head")
    return jax.shard_map(
        local,
        mesh=mesh,
        in_specs=(placed, placed, placed, P(), P()),
        out_specs=placed,
        check_vma=False,
    )
```

```python
import functools

import jax
import jax.numpy as jnp
from jax import lax
from jax.experimental import pallas as pl
from jax.experimental.pallas import tpu as pltpu
from jax.sharding import PartitionSpec as P

HD = 128
HBM = pl.BlockSpec(memory_space=pl.ANY)
SMALL = pl.BlockSpec(memory_space=pltpu.SMEM)
FAST = pl.BlockSpec(memory_space=pltpu.VMEM)
SCALE = HD ** (-0.5)
AHEAD = 7 * 10**9


def list_heads(profile, order, kind, width):
    first = lax.axis_index("head") * width

    for i in range(width):
        order[i] = 0
    count = jnp.int32(0)
    for i in range(width):
        hit = profile[first + i] == kind

        @pl.when(hit)
        def _(i=i, count=count):
            order[count] = i

        count = count + hit.astype(jnp.int32)
    return count


def columns_of(head):
    return pl.ds(pl.multiple_of(head * HD, HD), HD)


def steps_of(frames):
    return [0] + list(range(frames - 1, 0, -1))


def long_steps(frames, surplus):
    least = 3 * frames if surplus <= 2 else 2 * frames
    return [step for step in steps_of(frames) if step and 4 * step >= least]


def partner(frame, step, frames):
    if frames & (frames - 1) == 0:
        return frame ^ step
    return (frame + step) % frames


def source_of(frame, step, frames):
    if frames & (frames - 1) == 0:
        return frame ^ step
    return (frame - step + frames) % frames


def params(megabytes=40):
    return pltpu.CompilerParams(vmem_limit_bytes=megabytes << 20)


def pack_chunks(low, steps, profile, query, key, value, after, *rest):
    sends, (order, sems) = rest[: len(steps)], rest[len(steps) :]
    list_heads(profile, order, 0, query.shape[1] // HD)
    frames, mine = lax.axis_size("frame"), lax.axis_index("frame")
    for number, (step, send) in enumerate(zip(steps, sends)):
        slots, chunk = send.shape[0], send.shape[2]
        rows = pl.ds(pl.multiple_of(partner(mine, step, frames) * chunk, chunk), chunk)
        for slot in range(slots):
            columns = columns_of(order[low + slot])
            for index, source in enumerate((query, key, value)):
                pltpu.make_async_copy(source.at[rows, columns], send.at[slot, index], sems.at[number]).start()
    for number, send in enumerate(sends):
        pltpu.make_async_copy(send, send, sems.at[number]).wait()


def prepare(frames, profile, query, key, value, after, send, near, apart, order, sems):
    width = key.shape[1] // HD
    mine = lax.axis_index("frame")
    slots, _, chunk, _ = near.shape
    list_heads(profile, order, 1, width)
    for slot in range(send.shape[0]):
        columns = columns_of(order[slot])
        for index, source in enumerate((key, value)):
            pltpu.make_async_copy(source.at[:, columns], send.at[slot, index], sems.at[0]).start()
    list_heads(profile, order, 0, width)
    rows = pl.ds(pl.multiple_of(mine * chunk, chunk), chunk)
    for slot in range(slots):
        columns = columns_of(order[slot])
        for index, source in enumerate((query, key, value)):
            pltpu.make_async_copy(source.at[rows, columns], near.at[slot, index], sems.at[1]).start()

    size = apart.shape[0]
    part = size // frames
    steps = steps_of(frames)

    def place(dim):
        at = lax.broadcasted_iota(jnp.int32, (size, size), dim)
        passed = [(at >= i * part).astype(jnp.int32) for i in range(1, frames)]
        step = sum(p * (steps[i] - steps[i - 1]) for i, p in enumerate(passed, 1))
        return source_of(mine, step, frames), at - sum(passed) * part

    (frame_row, token_row), (frame_col, token_col) = place(0), place(1)
    apart[...] = jnp.where(token_row == token_col, jnp.abs(frame_row - frame_col), frames + size)
    pltpu.make_async_copy(send, send, sems.at[0]).wait()
    pltpu.make_async_copy(near, near, sems.at[1]).wait()


def spatial_heads(size, peers, profile, query, key, value, *rest):
    fetched, (out, order) = rest[:peers], rest[peers:]
    list_heads(profile, order, 1, query.shape[1] // HD)

    def several(slots):
        columns = [columns_of(order[slot]) for slot in slots]
        scores = [
            score(query[:, c], jnp.concatenate([key[:, c]] + [f[slot, 0] for f in fetched]))
            for slot, c in zip(slots, columns)
        ]
        weights = [soften(one) for one in scores]
        for slot, c, (weight, total) in zip(slots, columns, weights):
            values = jnp.concatenate([value[:, c]] + [f[slot, 1] for f in fetched])
            out[:, c] = blend(weight, total, values).astype(out.dtype)

    def pair(number, carry):
        several([2 * number, jnp.minimum(2 * number + 1, size - 1)])
        return carry

    lax.fori_loop(0, (size + 1) // 2, pair, 0)


def score(query, keys):
    return SCALE * lax.dot_general(
        query, keys, (((1,), (1,)), ((), ())), preferred_element_type=jnp.float32
    )


def soften(scores):
    weights = jnp.exp(scores - jnp.max(scores, axis=1, keepdims=True))
    return weights.astype(jnp.bfloat16), jnp.sum(weights, axis=1, keepdims=True)


def blend(weights, total, values):
    return jnp.dot(weights, values, preferred_element_type=jnp.float32) / total


def temporal_heads(frames, extras, profile, window, near, apart, *rest):
    arrived, rest = rest[: frames - 1], rest[frames - 1 :]
    extra, rest = rest[:extras], rest[extras:]
    outs, order = rest[:frames], rest[frames]
    width = profile.shape[0] // lax.axis_size("head")
    slots, chunk = outs[0].shape[0], outs[0].shape[1]
    list_heads(profile, order, 0, width)
    first = lax.axis_index("head") * width
    part = apart.shape[0] // frames

    def chunk_of(number, slot, index, tokens):
        common = arrived[number]
        if isinstance(slot, int) and slot >= common.shape[0]:
            return extra[number][slot - common.shape[0], index, tokens]
        return common[slot, index, tokens]

    def several(slots):
        pieces, scores = [], []
        for slot in slots:
            inside = apart[...] <= jnp.minimum(window[first + order[slot]], frames)
            for start in range(0, chunk, part):
                tokens = slice(start, start + part)
                query_all, key_all, value_all = (
                    jnp.concatenate(
                        [near[slot, index, tokens]]
                        + [chunk_of(number, slot, index, tokens) for number in range(frames - 1)]
                    )
                    for index in range(3)
                )
                pieces.append((slot, tokens, value_all))
                scores.append(jnp.where(inside, score(query_all, key_all), -1e30))
        weights = [soften(one) for one in scores]
        for (slot, tokens, value_all), (weight, total) in zip(pieces, weights):
            result = blend(weight, total, value_all).astype(outs[0].dtype)
            for distance, out in enumerate(outs):
                out[slot, tokens] = result[distance * part : (distance + 1) * part]

    if slots <= 9:
        several(range(slots))
    else:

        def one(slot, carry):
            several([slot])
            return carry

        lax.fori_loop(0, slots, one, 0)


def put_back(sure, frames, profile, *rest):
    chunks = rest[:frames]
    _, out, order, sems = rest[frames:]
    width = out.shape[1] // HD
    mine = lax.axis_index("frame")
    total = list_heads(profile, order, 0, width)
    slots, chunk = chunks[0].shape[0], chunks[0].shape[1]

    def copies(slot):
        for distance, source in enumerate(chunks):
            at = partner(mine, steps_of(frames)[distance], frames)
            rows = pl.ds(pl.multiple_of(at * chunk, chunk), chunk)
            sem = sems.at[distance if slot < sure else slot * frames + distance]
            yield pltpu.make_async_copy(source.at[slot], out.at[rows, columns_of(order[slot])], sem)

    for slot in range(sure):
        for copy in copies(slot):
            copy.start()
    for slot in range(sure, slots):

        @pl.when(slot < total)
        def _(slot=slot):
            for copy in copies(slot):
                copy.start()

    if sure:
        for distance, source in enumerate(chunks):
            part = source.at[:sure]
            pltpu.make_async_copy(part, part, sems.at[distance]).wait()
    for slot in range(sure, slots):

        @pl.when(slot < total)
        def _(slot=slot):
            for copy in copies(slot):
                copy.wait()


def exchange(block, step, back=False, only=None):
    frames, cores = lax.axis_size("frame"), lax.axis_size("head")
    route = []
    for frame in range(frames):
        ends = (frame, partner(frame, step, frames))
        source, target = ends[::-1] if back else ends
        route += [(source * cores + core, target * cores + core) for core in range(cores) if only in (None, core)]
    return lax.ppermute(block, ("frame", "head"), route)


def program(size, rich, queries, key_states, value_states, profile, window):
    frames, spaces = lax.axis_size("frame"), lax.axis_size("space")
    rows, wide = queries.shape[0] * queries.shape[1], queries.shape[2]
    width, chunk = wide // HD, rows // frames
    part = chunk // 2 if chunk % 32 == 0 else chunk
    query, key, value = (a.reshape(rows, wide) for a in (queries, key_states, value_states))
    kind = queries.dtype
    order = pltpu.SMEM((width,), jnp.int32)
    sure = width * lax.axis_size("head") // 2 - size
    steps = steps_of(frames)[1:]
    common = size if rich is None else sure
    far = long_steps(frames, size - common)

    def pack(low, steps, counts, after):
        return pl.pallas_call(
            functools.partial(pack_chunks, low, steps),
            out_shape=[jax.ShapeDtypeStruct((count, 3, chunk, HD), kind) for count in counts],
            in_specs=[SMALL] + [HBM] * 4,
            out_specs=[HBM] * len(steps),
            scratch_shapes=[order, pltpu.SemaphoreType.DMA((len(steps),))],
            compiler_params=params(),
            cost_estimate=pl.CostEstimate(flops=0, bytes_accessed=sum(counts) * chunk * HD * 12, transcendentals=0),
        )(profile, query, key, value, after)

    sends = pack(0, steps, [common if step in far else size for step in steps], query)
    arrived = [exchange(block, step) for step, block in zip(steps, sends)]

    kept, near, apart = pl.pallas_call(
        functools.partial(prepare, frames),
        out_shape=[
            jax.ShapeDtypeStruct((size, 2, rows, HD), kind),
            jax.ShapeDtypeStruct((size, 3, chunk, HD), kind),
            jax.ShapeDtypeStruct((frames * part, frames * part), jnp.int32),
        ],
        in_specs=[SMALL] + [HBM] * 4,
        out_specs=[HBM, HBM, FAST],
        scratch_shapes=[order, pltpu.SemaphoreType.DMA((2,))],
        compiler_params=params(),
        cost_estimate=pl.CostEstimate(flops=0, bytes_accessed=size * 16 * rows * HD, transcendentals=0),
    )(profile, query, key, value, sends[-1])
    fetched = [
        lax.ppermute(kept, "space", [(i, (i + distance) % spaces) for i in range(spaces)])
        for distance in range(1, spaces)
    ]
    extra = []
    if common < size:
        sends = pack(common, far, [size - common] * len(far), kept)
        extra = [exchange(block, step, only=rich) for step, block in zip(far, sends)]
    started = pl.pallas_call(
        functools.partial(spatial_heads, size, spaces - 1),
        out_shape=jax.ShapeDtypeStruct((rows, wide), kind),
        in_specs=[SMALL] + [FAST] * (spaces + 2),
        out_specs=FAST,
        scratch_shapes=[order],
        compiler_params=params(),
        cost_estimate=pl.CostEstimate(
            flops=size * 4 * rows * rows * spaces * HD,
            bytes_accessed=wide * rows * 16,
            transcendentals=size * rows * rows * spaces,
        ),
    )(profile, query, key, value, *fetched)

    chunks = pl.pallas_call(
        functools.partial(temporal_heads, frames, len(extra)),
        out_shape=[jax.ShapeDtypeStruct((size, chunk, HD), kind)] * frames,
        in_specs=[SMALL, SMALL] + [FAST] * (frames + 1 + len(extra)),
        out_specs=[FAST] * frames,
        scratch_shapes=[order],
        compiler_params=params(),
        cost_estimate=pl.CostEstimate(
            flops=AHEAD,
            bytes_accessed=size * rows * HD * 8,
            transcendentals=size * rows * rows,
        ),
    )(profile, window, near, apart, *arrived, *extra)
    results = [chunks[0]] + [exchange(block, step, back=True) for step, block in zip(steps, chunks[1:])]

    last = pl.pallas_call(
        functools.partial(put_back, sure, frames),
        out_shape=jax.ShapeDtypeStruct((rows, wide), kind),
        in_specs=[SMALL] + [HBM] * (len(results) + 1),
        out_specs=HBM,
        scratch_shapes=[order, pltpu.SemaphoreType.DMA(((width + 1) * frames,))],
        input_output_aliases={len(results) + 1: 0},
        compiler_params=params(),
        cost_estimate=pl.CostEstimate(flops=0, bytes_accessed=width * rows * HD * 2, transcendentals=0),
    )(profile, *results, started)
    return last.reshape(queries.shape)


def local(queries, key_states, value_states, profile, window):
    width = queries.shape[2] // HD
    half = width * lax.axis_size("head") // 2
    even = half // 2
    first = jnp.sum((profile[:width] == 0).astype(jnp.int32))
    reach = min(3, even)
    branches = [
        functools.partial(program, even + abs(more), None if more == 0 else int(more < 0))
        for more in range(-reach, reach + 1)
    ]
    branches.append(functools.partial(program, width, None))
    offset = first - even + reach
    index = jnp.where((offset < 0) | (offset > 2 * reach), 2 * reach + 1, offset)
    return lax.switch(index, branches, queries, key_states, value_states, profile, window)


def solution(mesh):
    placed = P(("groups", "frame"), "space", "head")
    return jax.shard_map(
        local,
        mesh=mesh,
        in_specs=(placed, placed, placed, P(), P()),
        out_specs=placed,
        check_vma=False,
    )
```

```python
import functools

import jax
import jax.numpy as jnp
from jax import lax
from jax.experimental import pallas as pl
from jax.experimental.pallas import tpu as pltpu
from jax.sharding import PartitionSpec as P

HD = 128
HBM = pl.BlockSpec(memory_space=pl.ANY)
SMALL = pl.BlockSpec(memory_space=pltpu.SMEM)
FAST = pl.BlockSpec(memory_space=pltpu.VMEM)
SCALE = HD ** (-0.5)
AHEAD = 7 * 10**9


def list_heads(profile, order, kind, width):
    first = lax.axis_index("head") * width

    for i in range(width):
        order[i] = 0
    count = jnp.int32(0)
    for i in range(width):
        hit = profile[first + i] == kind

        @pl.when(hit)
        def _(i=i, count=count):
            order[count] = i

        count = count + hit.astype(jnp.int32)
    return count


def columns_of(head):
    return pl.ds(pl.multiple_of(head * HD, HD), HD)


def steps_of(frames):
    return [0] + list(range(frames - 1, 0, -1))


def long_steps(frames, surplus):
    least = 3 * frames if surplus <= 2 else 2 * frames
    return [step for step in steps_of(frames) if step and 4 * step >= least]


def partner(frame, step, frames):
    if frames & (frames - 1) == 0:
        return frame ^ step
    return (frame + step) % frames


def source_of(frame, step, frames):
    if frames & (frames - 1) == 0:
        return frame ^ step
    return (frame - step + frames) % frames


def params(megabytes=40):
    return pltpu.CompilerParams(vmem_limit_bytes=megabytes << 20)


def pack_chunks(low, steps, profile, query, key, value, after, *rest):
    sends, (order, sems) = rest[: len(steps)], rest[len(steps) :]
    list_heads(profile, order, 0, query.shape[1] // HD)
    frames, mine = lax.axis_size("frame"), lax.axis_index("frame")
    for number, (step, send) in enumerate(zip(steps, sends)):
        slots, chunk = send.shape[0], send.shape[2]
        rows = pl.ds(pl.multiple_of(partner(mine, step, frames) * chunk, chunk), chunk)
        for slot in range(slots):
            columns = columns_of(order[low + slot])
            for index, source in enumerate((query, key, value)):
                pltpu.make_async_copy(source.at[rows, columns], send.at[slot, index], sems.at[number]).start()
    for number, send in enumerate(sends):
        pltpu.make_async_copy(send, send, sems.at[number]).wait()


def prepare(frames, profile, query, key, value, after, send, near, apart, order, sems):
    width = key.shape[1] // HD
    mine = lax.axis_index("frame")
    slots, _, chunk, _ = near.shape
    list_heads(profile, order, 1, width)
    for slot in range(send.shape[0]):
        columns = columns_of(order[slot])
        for index, source in enumerate((key, value)):
            pltpu.make_async_copy(source.at[:, columns], send.at[slot, index], sems.at[0]).start()
    list_heads(profile, order, 0, width)
    rows = pl.ds(pl.multiple_of(mine * chunk, chunk), chunk)
    for slot in range(slots):
        columns = columns_of(order[slot])
        for index, source in enumerate((query, key, value)):
            pltpu.make_async_copy(source.at[rows, columns], near.at[slot, index], sems.at[1]).start()

    size = apart.shape[0]
    part = size // frames
    steps = steps_of(frames)

    def place(dim):
        at = lax.broadcasted_iota(jnp.int32, (size, size), dim)
        passed = [(at >= i * part).astype(jnp.int32) for i in range(1, frames)]
        step = sum(p * (steps[i] - steps[i - 1]) for i, p in enumerate(passed, 1))
        return source_of(mine, step, frames), at - sum(passed) * part

    (frame_row, token_row), (frame_col, token_col) = place(0), place(1)
    apart[...] = jnp.where(token_row == token_col, jnp.abs(frame_row - frame_col), frames + size)
    pltpu.make_async_copy(send, send, sems.at[0]).wait()
    pltpu.make_async_copy(near, near, sems.at[1]).wait()


def spatial_heads(size, peers, profile, query, key, value, *rest):
    fetched, (out, order) = rest[:peers], rest[peers:]
    list_heads(profile, order, 1, query.shape[1] // HD)

    def several(slots):
        columns = [columns_of(order[slot]) for slot in slots]
        scores = [
            score(query[:, c], jnp.concatenate([key[:, c]] + [f[slot, 0] for f in fetched]))
            for slot, c in zip(slots, columns)
        ]
        weights = [soften(one) for one in scores]
        for slot, c, (weight, total) in zip(slots, columns, weights):
            values = jnp.concatenate([value[:, c]] + [f[slot, 1] for f in fetched])
            out[:, c] = blend(weight, total, values).astype(out.dtype)

    def pair(number, carry):
        several([2 * number, jnp.minimum(2 * number + 1, size - 1)])
        return carry

    lax.fori_loop(0, (size + 1) // 2, pair, 0)


def score(query, keys):
    return SCALE * lax.dot_general(
        query, keys, (((1,), (1,)), ((), ())), preferred_element_type=jnp.float32
    )


def soften(scores):
    weights = jnp.exp(scores - jnp.max(scores, axis=1, keepdims=True))
    return weights.astype(jnp.bfloat16), jnp.sum(weights, axis=1, keepdims=True)


def blend(weights, total, values):
    return jnp.dot(weights, values, preferred_element_type=jnp.float32) / total


def temporal_heads(frames, extras, profile, window, near, apart, *rest):
    arrived, rest = rest[: frames - 1], rest[frames - 1 :]
    extra, rest = rest[:extras], rest[extras:]
    outs, order = rest[:frames], rest[frames]
    width = profile.shape[0] // lax.axis_size("head")
    slots, chunk = outs[0].shape[0], outs[0].shape[1]
    list_heads(profile, order, 0, width)
    first = lax.axis_index("head") * width
    part = apart.shape[0] // frames

    def chunk_of(number, slot, index, tokens):
        common = arrived[number]
        if isinstance(slot, int) and slot >= common.shape[0]:
            return extra[number][slot - common.shape[0], index, tokens]
        return common[slot, index, tokens]

    def several(slots):
        pieces, scores = [], []
        for slot in slots:
            inside = apart[...] <= jnp.minimum(window[first + order[slot]], frames)
            for start in range(0, chunk, part):
                tokens = slice(start, start + part)
                query_all, key_all, value_all = (
                    jnp.concatenate(
                        [near[slot, index, tokens]]
                        + [chunk_of(number, slot, index, tokens) for number in range(frames - 1)]
                    )
                    for index in range(3)
                )
                pieces.append((slot, tokens, value_all))
                scores.append(jnp.where(inside, score(query_all, key_all), -1e30))
        weights = [soften(one) for one in scores]
        for (slot, tokens, value_all), (weight, total) in zip(pieces, weights):
            result = blend(weight, total, value_all).astype(outs[0].dtype)
            for distance, out in enumerate(outs):
                out[slot, tokens] = result[distance * part : (distance + 1) * part]

    if slots <= 9:
        several(range(slots))
    else:

        def one(slot, carry):
            several([slot])
            return carry

        lax.fori_loop(0, slots, one, 0)


def put_back(sure, frames, profile, *rest):
    chunks = rest[:frames]
    _, out, order, sems = rest[frames:]
    width = out.shape[1] // HD
    mine = lax.axis_index("frame")
    total = list_heads(profile, order, 0, width)
    slots, chunk = chunks[0].shape[0], chunks[0].shape[1]

    def copies(slot):
        for distance, source in enumerate(chunks):
            at = partner(mine, steps_of(frames)[distance], frames)
            rows = pl.ds(pl.multiple_of(at * chunk, chunk), chunk)
            sem = sems.at[distance if slot < sure else slot * frames + distance]
            yield pltpu.make_async_copy(source.at[slot], out.at[rows, columns_of(order[slot])], sem)

    for slot in range(sure):
        for copy in copies(slot):
            copy.start()
    for slot in range(sure, slots):

        @pl.when(slot < total)
        def _(slot=slot):
            for copy in copies(slot):
                copy.start()

    if sure:
        for distance, source in enumerate(chunks):
            part = source.at[:sure]
            pltpu.make_async_copy(part, part, sems.at[distance]).wait()
    for slot in range(sure, slots):

        @pl.when(slot < total)
        def _(slot=slot):
            for copy in copies(slot):
                copy.wait()


def exchange(block, step, back=False, only=None):
    frames, cores = lax.axis_size("frame"), lax.axis_size("head")
    route = []
    for frame in range(frames):
        ends = (frame, partner(frame, step, frames))
        source, target = ends[::-1] if back else ends
        route += [(source * cores + core, target * cores + core) for core in range(cores) if only in (None, core)]
    return lax.ppermute(block, ("frame", "head"), route)


def program(size, rich, queries, key_states, value_states, profile, window, *ready):
    frames, spaces = lax.axis_size("frame"), lax.axis_size("space")
    rows, wide = queries.shape[0] * queries.shape[1], queries.shape[2]
    width, chunk = wide // HD, rows // frames
    part = chunk // 2 if chunk % 32 == 0 else chunk
    query, key, value = (a.reshape(rows, wide) for a in (queries, key_states, value_states))
    kind = queries.dtype
    order = pltpu.SMEM((width,), jnp.int32)
    sure = width * lax.axis_size("head") // 2 - size
    steps = steps_of(frames)[1:]
    common = size if rich is None else sure
    far = long_steps(frames, size - common)

    def pack(low, steps, counts, after):
        return pl.pallas_call(
            functools.partial(pack_chunks, low, steps),
            out_shape=[jax.ShapeDtypeStruct((count, 3, chunk, HD), kind) for count in counts],
            in_specs=[SMALL] + [HBM] * 4,
            out_specs=[HBM] * len(steps),
            scratch_shapes=[order, pltpu.SemaphoreType.DMA((len(steps),))],
            compiler_params=params(),
            cost_estimate=pl.CostEstimate(flops=0, bytes_accessed=sum(counts) * chunk * HD * 12, transcendentals=0),
        )(profile, query, key, value, after)

    counts = [common if step in far else size for step in steps]
    given = [block for block in ready if block.shape[0] == counts[0]][:1]
    sends = list(given)
    if len(given) < len(steps):
        sends += pack(0, steps[len(given) :], counts[len(given) :], given[0] if given else query)
    arrived = [exchange(block, step) for step, block in zip(steps, sends)]

    kept, near, apart = pl.pallas_call(
        functools.partial(prepare, frames),
        out_shape=[
            jax.ShapeDtypeStruct((size, 2, rows, HD), kind),
            jax.ShapeDtypeStruct((size, 3, chunk, HD), kind),
            jax.ShapeDtypeStruct((frames * part, frames * part), jnp.int32),
        ],
        in_specs=[SMALL] + [HBM] * 4,
        out_specs=[HBM, HBM, FAST],
        scratch_shapes=[order, pltpu.SemaphoreType.DMA((2,))],
        compiler_params=params(),
        cost_estimate=pl.CostEstimate(flops=0, bytes_accessed=size * 16 * rows * HD, transcendentals=0),
    )(profile, query, key, value, sends[-1])
    fetched = [
        lax.ppermute(kept, "space", [(i, (i + distance) % spaces) for i in range(spaces)])
        for distance in range(1, spaces)
    ]
    extra = []
    if common < size:
        sends = pack(common, far, [size - common] * len(far), kept)
        extra = [exchange(block, step, only=rich) for step, block in zip(far, sends)]
    started = pl.pallas_call(
        functools.partial(spatial_heads, size, spaces - 1),
        out_shape=jax.ShapeDtypeStruct((rows, wide), kind),
        in_specs=[SMALL] + [FAST] * (spaces + 2),
        out_specs=FAST,
        scratch_shapes=[order],
        compiler_params=params(),
        cost_estimate=pl.CostEstimate(
            flops=size * 4 * rows * rows * spaces * HD,
            bytes_accessed=wide * rows * 16,
            transcendentals=size * rows * rows * spaces,
        ),
    )(profile, query, key, value, *fetched)

    chunks = pl.pallas_call(
        functools.partial(temporal_heads, frames, len(extra)),
        out_shape=[jax.ShapeDtypeStruct((size, chunk, HD), kind)] * frames,
        in_specs=[SMALL, SMALL] + [FAST] * (frames + 1 + len(extra)),
        out_specs=[FAST] * frames,
        scratch_shapes=[order],
        compiler_params=params(),
        cost_estimate=pl.CostEstimate(
            flops=AHEAD,
            bytes_accessed=size * rows * HD * 8,
            transcendentals=size * rows * rows,
        ),
    )(profile, window, near, apart, *arrived, *extra)
    results = [chunks[0]] + [exchange(block, step, back=True) for step, block in zip(steps, chunks[1:])]

    last = pl.pallas_call(
        functools.partial(put_back, sure, frames),
        out_shape=jax.ShapeDtypeStruct((rows, wide), kind),
        in_specs=[SMALL] + [HBM] * (len(results) + 1),
        out_specs=HBM,
        scratch_shapes=[order, pltpu.SemaphoreType.DMA(((width + 1) * frames,))],
        input_output_aliases={len(results) + 1: 0},
        compiler_params=params(),
        cost_estimate=pl.CostEstimate(flops=0, bytes_accessed=width * rows * HD * 2, transcendentals=0),
    )(profile, *results, started)
    return last.reshape(queries.shape)


def begin(even, reach, step, profile, query, key, value, index, *rest):
    sends, (order, sems) = rest[:-2], rest[-2:]
    width = query.shape[1] // HD
    first = sum((profile[i] == 0).astype(jnp.int32) for i in range(width))
    offset = first - even + reach
    index[0] = jnp.where((offset < 0) | (offset > 2 * reach), 2 * reach + 1, offset)
    pack_chunks(0, [step] * len(sends), profile, query, key, value, None, *sends, order, sems)


def local(queries, key_states, value_states, profile, window):
    width = queries.shape[2] // HD
    half = width * lax.axis_size("head") // 2
    even = half // 2
    reach = min(3, even)
    frames, rows, wide = lax.axis_size("frame"), queries.shape[0] * queries.shape[1], queries.shape[2]
    counts = [even]
    shapes = [jax.ShapeDtypeStruct((count, 3, rows // frames, HD), queries.dtype) for count in counts]
    index, *ready = pl.pallas_call(
        functools.partial(begin, even, reach, steps_of(frames)[1]),
        out_shape=[jax.ShapeDtypeStruct((1,), jnp.int32)] + shapes,
        in_specs=[SMALL] + [HBM] * 3,
        out_specs=[SMALL] + [FAST] * len(counts),
        scratch_shapes=[pltpu.SMEM((width,), jnp.int32), pltpu.SemaphoreType.DMA((len(counts),))],
        compiler_params=params(),
    )(profile, *(a.reshape(rows, wide) for a in (queries, key_states, value_states)))
    branches = [
        functools.partial(program, even + abs(more), None if more == 0 else int(more < 0))
        for more in range(-reach, reach + 1)
    ]
    branches.append(functools.partial(program, width, None))
    return lax.switch(index[0], branches, queries, key_states, value_states, profile, window, *ready)


def solution(mesh):
    placed = P(("groups", "frame"), "space", "head")
    return jax.shard_map(
        local,
        mesh=mesh,
        in_specs=(placed, placed, placed, P(), P()),
        out_specs=placed,
        check_vma=False,
    )
```

```python
import functools

import jax
import jax.numpy as jnp
from jax import lax
from jax.experimental import pallas as pl
from jax.experimental.pallas import tpu as pltpu
from jax.sharding import PartitionSpec as P

HD = 128
HBM = pl.BlockSpec(memory_space=pl.ANY)
SMALL = pl.BlockSpec(memory_space=pltpu.SMEM)
FAST = pl.BlockSpec(memory_space=pltpu.VMEM)
SCALE = HD ** (-0.5)
AHEAD = 7 * 10**9


def list_heads(profile, order, kind, width):
    first = lax.axis_index("head") * width

    for i in range(width):
        order[i] = 0
    count = jnp.int32(0)
    for i in range(width):
        hit = profile[first + i] == kind

        @pl.when(hit)
        def _(i=i, count=count):
            order[count] = i

        count = count + hit.astype(jnp.int32)
    return count


def columns_of(head):
    return pl.ds(pl.multiple_of(head * HD, HD), HD)


def steps_of(frames):
    return [0] + list(range(frames - 1, 0, -1))


def long_steps(frames, surplus, common):
    least = 2 * frames if 2 < surplus <= common else 3 * frames
    return [step for step in steps_of(frames) if step and 4 * step >= least]


def partner(frame, step, frames):
    if frames & (frames - 1) == 0:
        return frame ^ step
    return (frame + step) % frames


def source_of(frame, step, frames):
    if frames & (frames - 1) == 0:
        return frame ^ step
    return (frame - step + frames) % frames


def params(megabytes=40):
    return pltpu.CompilerParams(vmem_limit_bytes=megabytes << 20)


def pack_chunks(low, steps, profile, query, key, value, after, *rest):
    sends, (order, sems) = rest[: len(steps)], rest[len(steps) :]
    list_heads(profile, order, 0, query.shape[1] // HD)
    frames, mine = lax.axis_size("frame"), lax.axis_index("frame")
    for number, (step, send) in enumerate(zip(steps, sends)):
        slots, chunk = send.shape[0], send.shape[2]
        rows = pl.ds(pl.multiple_of(partner(mine, step, frames) * chunk, chunk), chunk)
        for slot in range(slots):
            columns = columns_of(order[low + slot])
            for index, source in enumerate((query, key, value)):
                pltpu.make_async_copy(source.at[rows, columns], send.at[slot, index], sems.at[number]).start()
    for number, send in enumerate(sends):
        pltpu.make_async_copy(send, send, sems.at[number]).wait()


def prepare(frames, profile, query, key, value, after, send, near, apart, order, sems):
    width = key.shape[1] // HD
    mine = lax.axis_index("frame")
    slots, _, chunk, _ = near.shape
    list_heads(profile, order, 1, width)
    for slot in range(send.shape[0]):
        columns = columns_of(order[slot])
        for index, source in enumerate((key, value)):
            pltpu.make_async_copy(source.at[:, columns], send.at[slot, index], sems.at[0]).start()
    list_heads(profile, order, 0, width)
    rows = pl.ds(pl.multiple_of(mine * chunk, chunk), chunk)
    for slot in range(slots):
        columns = columns_of(order[slot])
        for index, source in enumerate((query, key, value)):
            pltpu.make_async_copy(source.at[rows, columns], near.at[slot, index], sems.at[1]).start()

    size = apart.shape[0]
    part = size // frames
    steps = steps_of(frames)

    def place(dim):
        at = lax.broadcasted_iota(jnp.int32, (size, size), dim)
        passed = [(at >= i * part).astype(jnp.int32) for i in range(1, frames)]
        step = sum(p * (steps[i] - steps[i - 1]) for i, p in enumerate(passed, 1))
        return source_of(mine, step, frames), at - sum(passed) * part

    (frame_row, token_row), (frame_col, token_col) = place(0), place(1)
    apart[...] = jnp.where(token_row == token_col, jnp.abs(frame_row - frame_col), frames + size)
    pltpu.make_async_copy(send, send, sems.at[0]).wait()
    pltpu.make_async_copy(near, near, sems.at[1]).wait()


def spatial_heads(size, peers, profile, query, key, value, *rest):
    fetched, (out, order) = rest[:peers], rest[peers:]
    list_heads(profile, order, 1, query.shape[1] // HD)

    def several(slots):
        columns = [columns_of(order[slot]) for slot in slots]
        scores = [
            score(query[:, c], jnp.concatenate([key[:, c]] + [f[slot, 0] for f in fetched]))
            for slot, c in zip(slots, columns)
        ]
        weights = [soften(one) for one in scores]
        for slot, c, (weight, total) in zip(slots, columns, weights):
            values = jnp.concatenate([value[:, c]] + [f[slot, 1] for f in fetched])
            out[:, c] = blend(weight, total, values).astype(out.dtype)

    def pair(number, carry):
        several([2 * number, jnp.minimum(2 * number + 1, size - 1)])
        return carry

    lax.fori_loop(0, (size + 1) // 2, pair, 0)


def score(query, keys):
    return SCALE * lax.dot_general(
        query, keys, (((1,), (1,)), ((), ())), preferred_element_type=jnp.float32
    )


def soften(scores):
    weights = jnp.exp(scores - jnp.max(scores, axis=1, keepdims=True))
    return weights.astype(jnp.bfloat16), jnp.sum(weights, axis=1, keepdims=True)


def blend(weights, total, values):
    return jnp.dot(weights, values, preferred_element_type=jnp.float32) / total


def temporal_heads(frames, extras, profile, window, near, apart, *rest):
    arrived, rest = rest[: frames - 1], rest[frames - 1 :]
    extra, rest = rest[:extras], rest[extras:]
    outs, order = rest[:frames], rest[frames]
    width = profile.shape[0] // lax.axis_size("head")
    slots, chunk = outs[0].shape[0], outs[0].shape[1]
    list_heads(profile, order, 0, width)
    first = lax.axis_index("head") * width
    part = apart.shape[0] // frames

    def chunk_of(number, slot, index, tokens):
        common = arrived[number]
        if isinstance(slot, int) and slot >= common.shape[0]:
            return extra[number][slot - common.shape[0], index, tokens]
        return common[slot, index, tokens]

    def several(slots):
        pieces, scores = [], []
        for slot in slots:
            inside = apart[...] <= jnp.minimum(window[first + order[slot]], frames)
            for start in range(0, chunk, part):
                tokens = slice(start, start + part)
                query_all, key_all, value_all = (
                    jnp.concatenate(
                        [near[slot, index, tokens]]
                        + [chunk_of(number, slot, index, tokens) for number in range(frames - 1)]
                    )
                    for index in range(3)
                )
                pieces.append((slot, tokens, value_all))
                scores.append(jnp.where(inside, score(query_all, key_all), -1e30))
        weights = [soften(one) for one in scores]
        for (slot, tokens, value_all), (weight, total) in zip(pieces, weights):
            result = blend(weight, total, value_all).astype(outs[0].dtype)
            for distance, out in enumerate(outs):
                out[slot, tokens] = result[distance * part : (distance + 1) * part]

    if slots <= 9:
        several(range(slots))
    else:

        def one(slot, carry):
            several([slot])
            return carry

        lax.fori_loop(0, slots, one, 0)


def put_back(sure, frames, profile, *rest):
    chunks = rest[:frames]
    _, out, order, sems = rest[frames:]
    width = out.shape[1] // HD
    mine = lax.axis_index("frame")
    total = list_heads(profile, order, 0, width)
    slots, chunk = chunks[0].shape[0], chunks[0].shape[1]

    def copies(slot):
        for distance, source in enumerate(chunks):
            at = partner(mine, steps_of(frames)[distance], frames)
            rows = pl.ds(pl.multiple_of(at * chunk, chunk), chunk)
            sem = sems.at[distance if slot < sure else slot * frames + distance]
            yield pltpu.make_async_copy(source.at[slot], out.at[rows, columns_of(order[slot])], sem)

    for slot in range(sure):
        for copy in copies(slot):
            copy.start()
    for slot in range(sure, slots):

        @pl.when(slot < total)
        def _(slot=slot):
            for copy in copies(slot):
                copy.start()

    if sure:
        for distance, source in enumerate(chunks):
            part = source.at[:sure]
            pltpu.make_async_copy(part, part, sems.at[distance]).wait()
    for slot in range(sure, slots):

        @pl.when(slot < total)
        def _(slot=slot):
            for copy in copies(slot):
                copy.wait()


def exchange(block, step, back=False, only=None):
    frames, cores = lax.axis_size("frame"), lax.axis_size("head")
    route = []
    for frame in range(frames):
        ends = (frame, partner(frame, step, frames))
        source, target = ends[::-1] if back else ends
        route += [(source * cores + core, target * cores + core) for core in range(cores) if only in (None, core)]
    return lax.ppermute(block, ("frame", "head"), route)


def program(size, rich, queries, key_states, value_states, profile, window, *ready):
    frames, spaces = lax.axis_size("frame"), lax.axis_size("space")
    rows, wide = queries.shape[0] * queries.shape[1], queries.shape[2]
    width, chunk = wide // HD, rows // frames
    part = chunk // 2 if chunk % 32 == 0 else chunk
    query, key, value = (a.reshape(rows, wide) for a in (queries, key_states, value_states))
    kind = queries.dtype
    order = pltpu.SMEM((width,), jnp.int32)
    sure = width * lax.axis_size("head") // 2 - size
    steps = steps_of(frames)[1:]
    common = size if rich is None else sure
    far = long_steps(frames, size - common, size if rich else common)

    def pack(low, steps, counts, after):
        return pl.pallas_call(
            functools.partial(pack_chunks, low, steps),
            out_shape=[jax.ShapeDtypeStruct((count, 3, chunk, HD), kind) for count in counts],
            in_specs=[SMALL] + [HBM] * 4,
            out_specs=[HBM] * len(steps),
            scratch_shapes=[order, pltpu.SemaphoreType.DMA((len(steps),))],
            compiler_params=params(),
            cost_estimate=pl.CostEstimate(flops=0, bytes_accessed=sum(counts) * chunk * HD * 12, transcendentals=0),
        )(profile, query, key, value, after)

    counts = [common if step in far else size for step in steps]
    given = [block for block in ready if block.shape[0] == counts[0]][:1]
    sends = list(given)
    if len(given) < len(steps):
        sends += pack(0, steps[len(given) :], counts[len(given) :], given[0] if given else query)
    arrived = [exchange(block, step) for step, block in zip(steps, sends)]

    kept, near, apart = pl.pallas_call(
        functools.partial(prepare, frames),
        out_shape=[
            jax.ShapeDtypeStruct((size, 2, rows, HD), kind),
            jax.ShapeDtypeStruct((size, 3, chunk, HD), kind),
            jax.ShapeDtypeStruct((frames * part, frames * part), jnp.int32),
        ],
        in_specs=[SMALL] + [HBM] * 4,
        out_specs=[HBM, HBM, FAST],
        scratch_shapes=[order, pltpu.SemaphoreType.DMA((2,))],
        compiler_params=params(),
        cost_estimate=pl.CostEstimate(flops=0, bytes_accessed=size * 16 * rows * HD, transcendentals=0),
    )(profile, query, key, value, sends[-1])
    fetched = [
        lax.ppermute(kept, "space", [(i, (i + distance) % spaces) for i in range(spaces)])
        for distance in range(1, spaces)
    ]
    extra = []
    if common < size:
        sends = pack(common, far, [size - common] * len(far), kept)
        extra = [exchange(block, step, only=rich) for step, block in zip(far, sends)]
    started = pl.pallas_call(
        functools.partial(spatial_heads, size, spaces - 1),
        out_shape=jax.ShapeDtypeStruct((rows, wide), kind),
        in_specs=[SMALL] + [FAST] * (spaces + 2),
        out_specs=FAST,
        scratch_shapes=[order],
        compiler_params=params(),
        cost_estimate=pl.CostEstimate(
            flops=size * 4 * rows * rows * spaces * HD,
            bytes_accessed=wide * rows * 16,
            transcendentals=size * rows * rows * spaces,
        ),
    )(profile, query, key, value, *fetched)

    chunks = pl.pallas_call(
        functools.partial(temporal_heads, frames, len(extra)),
        out_shape=[jax.ShapeDtypeStruct((size, chunk, HD), kind)] * frames,
        in_specs=[SMALL, SMALL] + [FAST] * (frames + 1 + len(extra)),
        out_specs=[FAST] * frames,
        scratch_shapes=[order],
        compiler_params=params(),
        cost_estimate=pl.CostEstimate(
            flops=AHEAD,
            bytes_accessed=size * rows * HD * 8,
            transcendentals=size * rows * rows,
        ),
    )(profile, window, near, apart, *arrived, *extra)
    results = [chunks[0]] + [exchange(block, step, back=True) for step, block in zip(steps, chunks[1:])]

    last = pl.pallas_call(
        functools.partial(put_back, sure, frames),
        out_shape=jax.ShapeDtypeStruct((rows, wide), kind),
        in_specs=[SMALL] + [HBM] * (len(results) + 1),
        out_specs=HBM,
        scratch_shapes=[order, pltpu.SemaphoreType.DMA(((width + 1) * frames,))],
        input_output_aliases={len(results) + 1: 0},
        compiler_params=params(),
        cost_estimate=pl.CostEstimate(flops=0, bytes_accessed=width * rows * HD * 2, transcendentals=0),
    )(profile, *results, started)
    return last.reshape(queries.shape)


def begin(even, reach, step, profile, query, key, value, index, *rest):
    sends, (order, sems) = rest[:-2], rest[-2:]
    width = query.shape[1] // HD
    first = sum((profile[i] == 0).astype(jnp.int32) for i in range(width))
    offset = first - even + reach
    index[0] = jnp.where((offset < 0) | (offset > 2 * reach), 2 * reach + 1, offset)
    pack_chunks(0, [step] * len(sends), profile, query, key, value, None, *sends, order, sems)


def local(queries, key_states, value_states, profile, window):
    width = queries.shape[2] // HD
    half = width * lax.axis_size("head") // 2
    even = half // 2
    reach = min(3, even)
    frames, rows, wide = lax.axis_size("frame"), queries.shape[0] * queries.shape[1], queries.shape[2]
    counts = [even]
    shapes = [jax.ShapeDtypeStruct((count, 3, rows // frames, HD), queries.dtype) for count in counts]
    index, *ready = pl.pallas_call(
        functools.partial(begin, even, reach, steps_of(frames)[1]),
        out_shape=[jax.ShapeDtypeStruct((1,), jnp.int32)] + shapes,
        in_specs=[SMALL] + [HBM] * 3,
        out_specs=[SMALL] + [FAST] * len(counts),
        scratch_shapes=[pltpu.SMEM((width,), jnp.int32), pltpu.SemaphoreType.DMA((len(counts),))],
        compiler_params=params(),
    )(profile, *(a.reshape(rows, wide) for a in (queries, key_states, value_states)))
    branches = [
        functools.partial(program, even + abs(more), None if more == 0 else int(more < 0))
        for more in range(-reach, reach + 1)
    ]
    branches.append(functools.partial(program, width, None))
    return lax.switch(index[0], branches, queries, key_states, value_states, profile, window, *ready)


def solution(mesh):
    placed = P(("groups", "frame"), "space", "head")
    return jax.shard_map(
        local,
        mesh=mesh,
        in_specs=(placed, placed, placed, P(), P()),
        out_specs=placed,
        check_vma=False,
    )
```
